256 devices in a mesh: group: 16 (over z, x_hi), tp: 16 (over x_lo, y, core).
Axes of the slice: x: 4 (x_hi: 2, x_lo: 2; x = x_hi * 2 + x_lo), y: 4, z: 8, core: 2. Of those that a mesh axis runs over, the one named last changes fastest.
Arguments:
- hidden_in: bfloat16 [16, 8, 4, 5120], P('group'), may hold values from -6 to 6
- q_weight: bfloat16 [5120, 4096], P(None, 'tp'), may hold values from -0.078125 to 0.078125
- kv_weight: bfloat16 [5120, 1024], P(None, 'tp'), may hold values from -0.078125 to 0.078125
- o_weight: bfloat16 [4096, 5120], P('tp'), may hold values from -0.09375 to 0.09375
- q_gain: float32 [128], replicated, may hold values from 1 to 8
- k_gain: float32 [128], replicated, may hold values from 1 to 8
- cache: bfloat16 [16, 8, 2, 4, 4096, 128], P('group', None, None, None, 'tp'), may hold values from -6 to 6
- lengths: int32 [16, 8], P('group'), may hold values from 1 to 4092, 16384 in all within a row
- owner: int32 [16], replicated, may hold values from 0 to 15, each once
- a_q: bfloat16 [5120, 64], P('group'), may hold values from -0.078125 to 0.078125
- b_q: bfloat16 [64, 4096], P('group', 'tp'), may hold values from -0.75 to 0.75
- a_o: bfloat16 [4096, 64], P('tp', 'group'), may hold values from -0.09375 to 0.09375
- b_o: bfloat16 [64, 5120], P('group', 'tp'), may hold values from -0.75 to 0.75
Outputs:
- attn_out: bfloat16 [16, 8, 4, 5120], P('group', None, None, 'tp')
The draws below stay inside these ranges and needn't reach their ends.
Inputs may be any that keep to these rules, and one draw needn't show every extreme that they name: In each group the sequences' lengths sum to 16384 and the largest is 4092. `owner`: a permutation of the group indices.
All inputs are finite; a program needn't handle non-finite values.
Results may differ from the reference program's by a relative error of at most 0.012.
Values may be sent and summed in bfloat16 or wider, within the bound.
No kernel may reach another device: no remote copies, remote signals or barrier semaphores. Data moves between devices by JAX's collectives and lax.ppermute only.
A program may use at most 64 MiB of HBM per device.

```python
import math
import jax
import jax.numpy as jnp
import numpy as np
from jax import lax

D = 5120
HD = 128
QH = 32
KVH = 4
R = 64
STEPS = 4
SEQS = 8
CTX = 4096
N_GROUP = 16


def level_of(key, extent, cuts, low, top_value):
    def one(position, shards_of):
        steps = jax.random.uniform(jax.random.fold_in(jax.random.fold_in(key, 6), position), (shards_of,), jnp.float32, low / len(cuts), top_value / len(cuts))
        return jnp.repeat(jnp.exp(steps), extent[position] // shards_of).reshape((-1,) + (1,) * (len(extent) - position - 1))

    loudness = one(*cuts[0])
    for cut in cuts[1:]:
        loudness = loudness * one(*cut)
    return loudness


def split_up(count, total, limit, slope):
    weights = [(1 << 20) // math.isqrt(grade ** slope) + 1 for grade in range(2, count + 1)]
    surplus, holding = total - limit - (count - 1), [1] * (count - 1)
    while surplus > 0:
        free = [i for i in range(count - 1) if holding[i] < limit]
        whole, remaining = sum([weights[i] for i in free]), surplus
        for i in free:
            addition = min(limit - holding[i], max(1, remaining * weights[i] // whole), surplus)
            holding[i] = holding[i] + addition
            surplus = surplus - addition
    return np.array([limit] + holding)


def ragged(rng, amount, total, bound, lean):
    if amount == 2:
        one = jax.random.randint(rng, (), max(1, total - bound), min(bound, total - 1) + 1)
        return jnp.stack([one, total - one])
    sizes = jnp.asarray(split_up(amount, total, bound, lean), jnp.int32)
    pairs = (amount - 1) // 2
    giver, sink = sizes[1:1 + 2 * pairs:2], sizes[2:2 + 2 * pairs:2]
    room = jnp.minimum(giver - 1, bound - sink)
    moved = jax.random.randint(jax.random.fold_in(rng, 1), (pairs,), 0, 1 << 20) % (room + 1)
    sizes = sizes.at[1:1 + 2 * pairs:2].set(giver - moved).at[2:2 + 2 * pairs:2].set(sink + moved)
    return sizes[jax.random.permutation(jax.random.fold_in(rng, 2), amount)]


def scatter_about(own_key, dims, scale, most, shards=(), held_as=jnp.bfloat16):
    drawn = jax.random.normal(own_key, dims, jnp.float32) * scale
    if len(shards) > 0:
        drawn = level_of(own_key, dims, shards, -0.22, 0.18) * drawn
    return jnp.clip(drawn, min=-most, max=most).astype(held_as)


def setup_inputs(seed: int = 0) -> dict:
    keys = jax.random.split(jax.random.key(seed), 14)
    hidden_in = scatter_about(keys[0], (N_GROUP, SEQS, STEPS, D), 1.0, 6.0, ((0, 16),))
    q_weight = scatter_about(keys[1], (D, QH * HD), D ** -0.5, 0.078125, ((1, 16),))
    kv_weight = scatter_about(keys[2], (D, 2 * KVH * HD), D ** -0.5, 0.078125, ((1, 16),))
    o_weight = scatter_about(keys[3], (QH * HD, D), (QH * HD) ** -0.5, 0.09375, ((0, 16),))
    q_gain = jnp.clip(jnp.exp(jax.random.uniform(keys[4], (HD,), jnp.float32, math.log(1.0), math.log(8.0))), 1.0, 8.0)
    k_gain = jnp.clip(jnp.exp(jax.random.uniform(keys[5], (HD,), jnp.float32, math.log(1.0), math.log(8.0))), 1.0, 8.0)
    cache = scatter_about(keys[6], (N_GROUP, SEQS, 2, KVH, CTX, HD), 1.0, 6.0, ((0, 16), (4, 16)))
    lengths = jax.vmap(lambda own: ragged(own, SEQS, SEQS * CTX // 2, CTX - STEPS, 2))(jax.random.split(keys[7], N_GROUP)).reshape((N_GROUP, SEQS)).astype(jnp.int32)
    owner = jax.random.permutation(keys[8], N_GROUP).astype(jnp.int32)
    a_q = scatter_about(keys[9], (D, R), D ** -0.5, 0.078125, ((0, 16),))
    b_q = scatter_about(keys[10], (R, QH * HD), R ** -0.5, 0.75, ((0, 16), (1, 16)))
    a_o = scatter_about(keys[11], (QH * HD, R), (QH * HD) ** -0.5, 0.09375, ((0, 16), (1, 16)))
    b_o = scatter_about(keys[12], (R, D), R ** -0.5, 0.75, ((0, 16), (1, 16)))
    return dict(hidden_in=hidden_in, q_weight=q_weight, kv_weight=kv_weight, o_weight=o_weight, q_gain=q_gain, k_gain=k_gain, cache=cache, lengths=lengths, owner=owner, a_q=a_q, b_q=b_q, a_o=a_o, b_o=b_o)


def scaled_norm(values, gain_vec):
    mean_square = lax.optimization_barrier(jnp.mean(values * values, axis=-1, keepdims=True))
    return values * lax.rsqrt(mean_square + 1e-06) * gain_vec

def per_group(tokens, cache_group, length_group, q_weight, kv_weight, o_weight, q_gain, k_gain, a_true, b_q, a_o, b_o):
    row_count = SEQS * STEPS
    tokens = tokens.reshape(row_count, D)
    low_query = jnp.dot(tokens, a_true, preferred_element_type=jnp.float32)
    query_raw = jnp.dot(tokens, q_weight, preferred_element_type=jnp.float32) + 0.5 * jnp.dot(low_query, b_q.astype(jnp.float32), precision=lax.Precision.HIGHEST)
    keyval = jnp.dot(tokens, kv_weight, preferred_element_type=jnp.float32)
    queries = scaled_norm(query_raw.reshape(SEQS, STEPS, QH, HD), q_gain).astype(jnp.bfloat16)
    new_keys = scaled_norm(keyval[:, :KVH * HD].reshape(SEQS, STEPS, KVH, HD), k_gain).astype(jnp.bfloat16)
    new_values = keyval[:, KVH * HD:].reshape(SEQS, STEPS, KVH, HD).astype(jnp.bfloat16)
    grouped = queries.reshape(SEQS, STEPS, KVH, QH // KVH, HD).astype(jnp.float32)
    inv_root = 1.0 / math.sqrt(HD)
    cache_scores = jnp.einsum('stcgh,scph->stcgp', grouped, cache_group[:, 0].astype(jnp.float32)) * inv_root
    is_valid = jnp.arange(CTX, dtype=jnp.int32)[None, :] < length_group[:, None]
    cache_scores = jnp.where(is_valid[:, None, None, None, :], cache_scores, -jnp.inf)
    fresh_scores = jnp.einsum('stcgh,such->stcgu', grouped, new_keys.astype(jnp.float32)) * inv_root
    causal = jnp.arange(STEPS)[:, None] >= jnp.arange(STEPS)[None, :]
    fresh_scores = jnp.where(causal[None, :, None, None, :], fresh_scores, -jnp.inf)
    largest = jnp.maximum(cache_scores.max(-1), fresh_scores.max(-1))
    cache_weights = jnp.exp(cache_scores - largest[..., None])
    fresh_weights = jnp.exp(fresh_scores - largest[..., None])
    sum_total = cache_weights.sum(-1) + fresh_weights.sum(-1)
    weighted = jnp.einsum('stcgp,scph->stcgh', cache_weights.astype(jnp.bfloat16).astype(jnp.float32), cache_group[:, 1].astype(jnp.float32))
    weighted = weighted + jnp.einsum('stcgu,such->stcgh', fresh_weights.astype(jnp.bfloat16).astype(jnp.float32), new_values.astype(jnp.float32))
    attended = (weighted / sum_total[..., None]).reshape(row_count, QH * HD).astype(jnp.bfloat16)
    low_out = jnp.dot(attended, a_o, preferred_element_type=jnp.float32)
    result = jnp.dot(attended, o_weight, preferred_element_type=jnp.float32) + 0.5 * jnp.dot(low_out, b_o.astype(jnp.float32), precision=lax.Precision.HIGHEST)
    return result.astype(jnp.bfloat16).reshape(SEQS, STEPS, D)

def reference(hidden_in, q_weight, kv_weight, o_weight, q_gain, k_gain, cache, lengths, owner, a_q, b_q, a_o, b_o):
    block_rows = D // N_GROUP
    pieces = a_q.reshape(N_GROUP, block_rows, R)
    a_true = jnp.zeros_like(pieces).at[owner].set(pieces).reshape(D, R)

    def apply_group(packed):
        return per_group(packed[0], packed[1], packed[2], q_weight, kv_weight, o_weight, q_gain, k_gain, a_true, b_q, a_o, b_o)
    return lax.map(apply_group, (hidden_in, cache, lengths))
```

```python
import functools
import math

import jax
import jax.numpy as jnp
from jax import lax
from jax.experimental import pallas as pl
from jax.experimental.pallas import tpu as pltpu
from jax.sharding import PartitionSpec as P

HD = 128
QH = 32
KVH = 4
R = 64
TP = 16
GROUPS = 16
SEQS = 8
STEPS = 4
ROWS = SEQS * STEPS
PER_SEQ = 2 * STEPS
WIDTH = 5120
SLOTS = 256
BLOCK = WIDTH // GROUPS
HALF = BLOCK // 2
OUT = WIDTH // TP
INV_ROOT = 1.0 / math.sqrt(HD)
FAR = -1e30
BF16 = jnp.bfloat16
F32 = jnp.float32

BQ_AT = 80
AO_AT = 88
BO_AT = 96
FACTOR_ROWS = 112
QKV_ROWS = 96
PART_ROWS = 80

VMEM = pl.BlockSpec(memory_space=pltpu.VMEM)
SMEM = pl.BlockSpec(memory_space=pltpu.SMEM)
NT = (((1,), (1,)), ((), ()))


def lanes(shape):
    return lax.broadcasted_iota(jnp.int32, shape, len(shape) - 1)


def norm(values, gain):
    mean_square = jnp.mean(values * values, axis=-1, keepdims=True)
    return values * lax.rsqrt(mean_square + 1e-06) * gain


def pack_factors(a_q, b_q, a_o, b_o, out, rows):
    start = pl.multiple_of((lax.axis_index("tp") % 2) * HALF, HALF)
    first = a_q[pl.ds(start, 80), :].astype(F32)
    second = a_q[pl.ds(start + 80, 80), :].astype(F32)
    rows[0:80, :] = jnp.concatenate([first, second], axis=1)
    bq = b_q[...].astype(F32)
    rows[BQ_AT : BQ_AT + 4, :] = bq[:, :HD]
    rows[BQ_AT + 4 : BQ_AT + 8, :] = bq[:, HD:]
    unit = lax.broadcasted_iota(jnp.int32, (256, 256), 0) == lanes((256, 256))
    ao = lax.dot_general(
        a_o[...], unit.astype(F32).astype(BF16), (((0,), (0,)), ((), ())), preferred_element_type=F32
    )
    rows[AO_AT : AO_AT + 4, :] = ao[:, :HD]
    rows[AO_AT + 4 : AO_AT + 8, :] = ao[:, HD:]
    bo = b_o[...].astype(F32)
    rows[BO_AT : BO_AT + 4, :] = bo[:, :HD]
    rows[BO_AT + 4 : BO_AT + 8, :] = bo[:, HD : 2 * HD]
    rows[BO_AT + 8 : BO_AT + 16, :] = jnp.zeros((8, HD), F32)
    rows[BO_AT + 8 : BO_AT + 12, 0:64] = bo[:, 2 * HD :]
    message = rows[...].astype(BF16)
    for g in range(GROUPS):
        out[g] = message


def low_rank(owner, tokens, factors, out, a_true):
    core = lax.axis_index("tp") % 2
    lane = lanes((80, HD))
    left = jnp.where(lane < R, 1.0, 0.0).astype(BF16)
    right = jnp.where(lane < R, 0.0, 1.0).astype(BF16)
    empty = jnp.zeros((HALF, HD), BF16)
    for g in range(GROUPS):
        base = owner[g] * BLOCK
        mine = pl.multiple_of(base + core * HALF, 32)
        other = pl.multiple_of(base + (1 - core) * HALF, 32)
        block = factors[g, 0:80, :]
        a_true[pl.ds(mine, 80), :] = block * left
        a_true[pl.ds(pl.multiple_of(mine + 80, 16), 80), :] = block * right
        a_true[pl.ds(other, HALF), :] = empty
    both = jnp.dot(tokens[...], a_true[...], preferred_element_type=F32)
    out[...] = both + pltpu.roll(both, R, 1)


def unpack_factors(factors, bq_out, ao_out, bo_out, rows):
    for at, pieces, out in ((BQ_AT, 2, bq_out), (AO_AT, 2, ao_out), (BO_AT, 3, bo_out)):
        for g in range(GROUPS):
            block = factors[g, BQ_AT:FACTOR_ROWS, :].astype(F32)
            for h in range(pieces):
                piece = block[at - BQ_AT + 4 * h : at - BQ_AT + 4 * h + 4]
                rows[4 * g : 4 * g + 4, HD * h : HD * h + HD] = piece
        whole = rows[:, : HD * pieces].astype(BF16)
        out[0:R, :] = whole
        out[R : 2 * R, :] = whole


def pack_queries(query_part, keyval_part, low_own, low_other, bq, q_gain, out, rows):
    low = low_own[...] + low_other[...]
    lane = lanes((ROWS, HD))
    high = low.astype(BF16).astype(F32)
    low_terms = jnp.where(lane < R, high, low - high).astype(BF16)
    query = query_part[...] + 0.5 * jnp.dot(low_terms, bq[...], preferred_element_type=F32)
    for e in range(2):
        normed = norm(query[:, HD * e : HD * e + HD], q_gain[...])
        for s in range(SEQS):
            at = PER_SEQ * s + STEPS * e
            rows[at : at + STEPS, :] = normed[STEPS * s : STEPS * s + STEPS]
    keyval = keyval_part[...]
    high = keyval.astype(BF16).astype(F32)
    rows[64:96, :] = jnp.concatenate([high, keyval - high], axis=1)
    message = rows[...].astype(BF16)
    for i in range(TP):
        out[i] = message


def cached_attention(lengths, received, cache, out, queries, weighted):
    first = lax.axis_index("tp") * SLOTS
    for i in range(TP):
        queries[i] = received[i, 0:64, :].astype(F32)
    position = lanes((ROWS, SLOTS)) + first
    lane = lanes((ROWS, HD))
    for c in range(KVH):
        logs = jnp.zeros((ROWS, HD), F32)
        for s in range(SEQS):
            rows = pl.ds(PER_SEQ * s, PER_SEQ)
            query = queries[4 * c : 4 * c + 4, rows, :].reshape(ROWS, HD).astype(BF16)
            scores = (
                lax.dot_general(query, cache[0, s, 0, c], NT, preferred_element_type=F32) * INV_ROOT
            )
            valid = position < lengths[0, s]
            scores = jnp.where(valid, scores, FAR)
            largest = scores.max(axis=-1, keepdims=True)
            weights = jnp.where(valid, jnp.exp(scores - largest), 0.0)
            total = weights.sum(axis=-1, keepdims=True)
            value = jnp.dot(weights.astype(BF16), cache[0, s, 1, c], preferred_element_type=F32)
            safe = jnp.where(total > 0.0, total, 1.0)
            value = value / safe
            log = jnp.where(total > 0.0, largest + jnp.log(safe), FAR)
            logs = jnp.where(lane % SEQS == s, log, logs)
            weighted[4 * c : 4 * c + 4, rows, :] = value.reshape(4, PER_SEQ, HD)
        high = logs.astype(BF16).astype(F32)
        middle = (logs - high).astype(BF16).astype(F32)
        terms = jnp.where(lane < 8, high, jnp.where(lane < 16, middle, logs - high - middle))
        weighted[4 * c : 4 * c + 4, 64:72, :] = terms.reshape(4, PER_SEQ, HD)
        weighted[4 * c : 4 * c + 4, 72:80, :] = jnp.zeros((4, 8, HD), F32)
    for i in range(TP):
        out[i] = weighted[i].astype(BF16)


def fresh_attention(received, k_gain, out, logs):
    me = lax.axis_index("tp")
    head = me // (TP // KVH)
    lane = lanes((ROWS, HD))

    def raw(left, right):
        pair = []
        for device in (left, right):
            terms = received[device, 64:96, :].astype(F32)
            pair.append(terms + pltpu.roll(terms, R, 1))
        return jnp.where(lane < R, pair[0], pair[1])

    keys = norm(raw(2 * head, 2 * head + 1), k_gain[...]).astype(BF16)
    values = raw(8 + 2 * head, 9 + 2 * head).astype(BF16)
    scores = (
        lax.dot_general(received[me, 0:64, :], keys, NT, preferred_element_type=F32) * INV_ROOT
    )
    row = lax.broadcasted_iota(jnp.int32, (64, ROWS), 0)
    column = lanes((64, ROWS))
    seen = (row // PER_SEQ == column // STEPS) & (row % STEPS >= column % STEPS)
    scores = jnp.where(seen, scores, FAR)
    largest = scores.max(axis=-1, keepdims=True)
    weights = jnp.where(seen, jnp.exp(scores - largest), 0.0)
    total = weights.sum(axis=-1, keepdims=True)
    value = jnp.dot(weights.astype(BF16), values, preferred_element_type=F32)
    out[...] = value / total
    log = largest + jnp.log(total)
    lane = lanes((PER_SEQ, HD))
    compact = jnp.zeros((PER_SEQ, HD), F32)
    for s in range(SEQS):
        compact = jnp.where(lane == s, log[PER_SEQ * s : PER_SEQ * s + PER_SEQ], compact)
    logs[...] = compact


def project(received, fresh, fresh_logs, ao, o_weight, out, attended):
    logs = []
    for i in range(TP):
        terms = received[i, 64:80, :].astype(F32)[0:8]
        logs.append(terms + pltpu.roll(terms, HD - 8, 1) + pltpu.roll(terms, HD - 16, 1))
    logs.append(fresh_logs[...])
    largest = functools.reduce(jnp.maximum, logs)
    shares = [jnp.exp(log - largest) for log in logs]
    inverse = 1.0 / functools.reduce(jnp.add, shares)
    shares = [share * inverse for share in shares]
    for pair in range(SEQS // 2):
        blocks = [received[i, 16 * pair : 16 * pair + 16, :].astype(F32) for i in range(TP)]
        for s in (2 * pair, 2 * pair + 1):
            at = PER_SEQ * s
            total = fresh[at : at + PER_SEQ, :] * shares[TP][:, s : s + 1]
            for i in range(TP):
                part = blocks[i][at - 16 * pair : at - 16 * pair + PER_SEQ]
                total = total + part * shares[i][:, s : s + 1]
            for e in range(2):
                attended[STEPS * s : STEPS * s + STEPS, HD * e : HD * e + HD] = total[
                    STEPS * e : STEPS * e + STEPS
                ]
    heads = attended[...].astype(BF16)
    low = lax.dot_general(heads, ao[...], NT, preferred_element_type=F32)
    lane = lanes((ROWS, HD))
    for k in range(TP // 2):
        at = 2 * OUT * k
        value = jnp.dot(heads, o_weight[:, at : at + 2 * OUT], preferred_element_type=F32)
        out[2 * k, :, 0 : 2 * HD] = value[:, 0 : 2 * HD].astype(BF16)
        middle = value[:, 2 * HD : 3 * HD]
        out[2 * k, :, 2 * HD : 3 * HD] = jnp.where(lane < R, middle, low).astype(BF16)
        out[2 * k + 1, :, 0:HD] = jnp.where(lane < R, low, middle).astype(BF16)
        out[2 * k + 1, :, HD : 3 * HD] = value[:, 3 * HD :].astype(BF16)


def finish(received, bo, out):
    odd = lax.axis_index("tp") % 2 == 1
    total = received[0].astype(F32)
    for i in range(1, TP):
        total = total + received[i].astype(F32)
    lane = lanes((ROWS, HD))
    low = jnp.where(
        odd,
        jnp.where(lane < R, total[:, :HD], 0.0),
        jnp.where(lane < R, 0.0, total[:, 2 * HD :]),
    )
    high = low.astype(BF16)
    rest = (low - high.astype(F32)).astype(BF16)
    extra = jnp.dot(high, bo[...], preferred_element_type=F32) + jnp.dot(
        rest, bo[...], preferred_element_type=F32
    )
    moved = pltpu.roll(total, 3 * HD - R, 1)
    result = (jnp.where(odd, moved, total) + 0.5 * extra)[:, :OUT].astype(BF16)
    for s in range(SEQS):
        out[0, s] = result[STEPS * s : STEPS * s + STEPS]


def call(kernel, in_specs, outs, scratch=(), cost=None):
    single = not isinstance(outs, (list, tuple))
    return pl.pallas_call(
        kernel,
        out_shape=outs,
        in_specs=in_specs,
        out_specs=VMEM if single else [VMEM] * len(outs),
        scratch_shapes=list(scratch),
        cost_estimate=pl.CostEstimate(
            flops=cost or 1_000_000, bytes_accessed=1_000_000, transcendentals=0
        ),
        compiler_params=pltpu.CompilerParams(vmem_limit_bytes=24 * 1024 * 1024),
    )


def shape(*dims, dtype=BF16):
    return jax.ShapeDtypeStruct(dims, dtype)


def per_device(
    hidden_in,
    q_weight,
    kv_weight,
    o_weight,
    q_gain,
    k_gain,
    cache,
    lengths,
    owner,
    a_q,
    b_q,
    a_o,
    b_o,
):
    tokens = hidden_in.reshape(ROWS, WIDTH)
    q_gain, k_gain = q_gain.reshape(1, HD), k_gain.reshape(1, HD)

    message = call(
        pack_factors,
        [VMEM] * 4,
        shape(GROUPS, FACTOR_ROWS, HD),
        [pltpu.VMEM((FACTOR_ROWS, HD), F32)],
    )(a_q, b_q, a_o, b_o)
    factors = lax.all_to_all(message, "group", 0, 0)

    query_part = jnp.dot(tokens, q_weight, preferred_element_type=F32)
    keyval_part = jnp.dot(tokens, kv_weight, preferred_element_type=F32)

    low_own = call(
        low_rank,
        [SMEM, VMEM, VMEM],
        shape(ROWS, HD, dtype=F32),
        [pltpu.VMEM((WIDTH, HD), BF16)],
    )(owner, tokens, factors)
    low_other = lax.ppermute(low_own, "tp", [(i, i ^ 1) for i in range(TP)])
    bq, ao, bo = call(
        unpack_factors,
        [VMEM],
        [shape(2 * R, 2 * HD), shape(2 * R, 2 * HD), shape(2 * R, 3 * HD)],
        [pltpu.VMEM((R, 3 * HD), F32)],
    )(factors)
    message = call(
        pack_queries,
        [VMEM] * 6,
        shape(TP, QKV_ROWS, HD),
        [pltpu.VMEM((QKV_ROWS, HD), F32)],
    )(query_part, keyval_part, low_own, low_other, bq, q_gain)
    received = lax.all_to_all(message, "tp", 0, 0)

    message = call(
        cached_attention,
        [SMEM, VMEM, VMEM],
        shape(TP, PART_ROWS, HD),
        [pltpu.VMEM((TP, 64, HD), F32), pltpu.VMEM((TP, PART_ROWS, HD), F32)],
    )(lengths, received, cache)
    parts = lax.all_to_all(message, "tp", 0, 0)
    fresh, fresh_logs = call(
        fresh_attention,
        [VMEM, VMEM],
        [shape(64, HD, dtype=F32), shape(PER_SEQ, HD, dtype=F32)],
    )(received, k_gain)

    message = call(
        project,
        [VMEM] * 5,
        shape(TP, ROWS, 3 * HD),
        [pltpu.VMEM((ROWS, 2 * HD), F32)],
    )(parts, fresh, fresh_logs, ao, o_weight)
    sums = lax.all_to_all(message, "tp", 0, 0)
    return call(finish, [VMEM, VMEM], shape(1, SEQS, STEPS, OUT))(sums, bo)


def solution(mesh):
    placed = (
        P("group", None, None, None),
        P(None, "tp"),
        P(None, "tp"),
        P("tp", None),
        P(),
        P(),
        P("group", None, None, None, "tp", None),
        P("group", None),
        P(),
        P("group", None),
        P("group", "tp"),
        P("tp", "group"),
        P("group", "tp"),
    )
    return jax.shard_map(
        per_device,
        mesh=mesh,
        in_specs=placed,
        out_specs=P("group", None, None, "tp"),
        check_vma=False,
    )
```

```python
import functools
import math

import jax
import jax.numpy as jnp
from jax import lax
from jax.experimental import pallas as pl
from jax.experimental.pallas import tpu as pltpu
from jax.sharding import PartitionSpec as P

HD = 128
QH = 32
KVH = 4
R = 64
TP = 16
CHIPS = TP // 2
GROUPS = 16
SEQS = 8
STEPS = 4
ROWS = SEQS * STEPS
PER_SEQ = 2 * STEPS
WIDTH = 5120
SLOTS = 256
BLOCK = WIDTH // GROUPS
HALF = BLOCK // 2
OUT = WIDTH // TP
INV_ROOT = 1.0 / math.sqrt(HD)
FAR = -1e30
BF16 = jnp.bfloat16
F32 = jnp.float32

BQ_AT = 80
AO_AT = 88
BO_AT = 96
FACTOR_ROWS = 112
QKV_ROWS = 96
PART_ROWS = 80

VMEM = pl.BlockSpec(memory_space=pltpu.VMEM)
HBM = pl.BlockSpec(memory_space=pltpu.HBM)
ANY = pl.BlockSpec(memory_space=pl.ANY)
SMEM = pl.BlockSpec(memory_space=pltpu.SMEM)
NT = (((1,), (1,)), ((), ()))


def lanes(shape):
    return lax.broadcasted_iota(jnp.int32, shape, len(shape) - 1)


def norm(values, gain):
    mean_square = jnp.mean(values * values, axis=-1, keepdims=True)
    return values * lax.rsqrt(mean_square + 1e-06) * gain


def pack_factors(a_q, b_q, a_o, b_o, out, a_q_in, b_q_in, a_o_in, b_o_in, turned, rows, sems):
    pairs = ((a_q, a_q_in), (b_q, b_q_in), (a_o, a_o_in), (b_o, b_o_in))
    copies = [
        pltpu.make_async_copy(source, place, sems.at[k]) for k, (source, place) in enumerate(pairs)
    ]
    for copy in copies:
        copy.start()
    for copy in copies:
        copy.wait()
    row = lax.broadcasted_iota(jnp.int32, (R, HD), 0)
    unit = jnp.where(lanes((R, HD)) % R == row, 1.0, 0.0).astype(BF16)
    turned[...] = lax.dot_general(
        a_q_in[...], unit, (((0,), (0,)), ((), ())), preferred_element_type=F32
    )
    start = pl.multiple_of((lax.axis_index("tp") % 2) * HALF, HALF)
    first = turned[pl.ds(start, 80), :]
    second = turned[pl.ds(start + 80, 80), :]
    rows[0:80, :] = jnp.where(lanes((80, HD)) < R, first, second)
    bq = b_q_in[...].astype(F32)
    rows[BQ_AT : BQ_AT + 4, :] = bq[:, :HD]
    rows[BQ_AT + 4 : BQ_AT + 8, :] = bq[:, HD:]
    ao = a_o_in[...].astype(F32)
    rows[AO_AT : AO_AT + 4, :] = ao[:, :HD]
    rows[AO_AT + 4 : AO_AT + 8, :] = ao[:, HD:]
    bo = b_o_in[...].astype(F32)
    rows[BO_AT : BO_AT + 4, :] = bo[:, :HD]
    rows[BO_AT + 4 : BO_AT + 8, :] = bo[:, HD : 2 * HD]
    rows[BO_AT + 8 : BO_AT + 16, :] = jnp.zeros((8, HD), F32)
    rows[BO_AT + 8 : BO_AT + 12, 0:64] = bo[:, 2 * HD :]
    message = rows[...].astype(BF16)
    for g in range(GROUPS):
        out[g] = message


def stage_cache(cache, _, out, sems):
    copies = [pltpu.make_async_copy(cache.at[0, s], out.at[0, s], sems.at[s]) for s in range(SEQS)]
    for copy in copies:
        copy.start()
    for copy in copies:
        copy.wait()


def low_rank(owner, tokens, factors, _, __, out, a_true):
    core = lax.axis_index("tp") % 2
    lane = lanes((80, HD))
    left = jnp.where(lane < R, 1.0, 0.0).astype(BF16)
    right = jnp.where(lane < R, 0.0, 1.0).astype(BF16)
    empty = jnp.zeros((HALF, HD), BF16)
    for g in range(GROUPS):
        base = owner[g] * BLOCK
        mine = pl.multiple_of(base + core * HALF, 32)
        other = pl.multiple_of(base + (1 - core) * HALF, 32)
        block = factors[g, 0:80, :]
        a_true[pl.ds(mine, 80), :] = block * left
        a_true[pl.ds(pl.multiple_of(mine + 80, 16), 80), :] = block * right
        a_true[pl.ds(other, HALF), :] = empty
    both = jnp.dot(tokens[...], a_true[...], preferred_element_type=F32)
    out[...] = both + pltpu.roll(both, R, 1)


def unpack_factors(factors, bq_out, ao_out, bo_out, rows):
    for at, pieces, out in ((BQ_AT, 2, bq_out), (AO_AT, 2, ao_out), (BO_AT, 3, bo_out)):
        for g in range(GROUPS):
            block = factors[g, BQ_AT:FACTOR_ROWS, :].astype(F32)
            for h in range(pieces):
                piece = block[at - BQ_AT + 4 * h : at - BQ_AT + 4 * h + 4]
                rows[4 * g : 4 * g + 4, HD * h : HD * h + HD] = piece
        whole = rows[:, : HD * pieces].astype(BF16)
        out[0:R, :] = whole
        out[R : 2 * R, :] = whole


def pack_queries(query_part, keyval_part, low_own, low_other, bq, gains, out, rows):
    low = low_own[...] + low_other[...]
    lane = lanes((ROWS, HD))
    high = low.astype(BF16).astype(F32)
    low_terms = jnp.where(lane < R, high, low - high).astype(BF16)
    query = query_part[...] + 0.5 * jnp.dot(low_terms, bq[...], preferred_element_type=F32)
    for e in range(2):
        normed = norm(query[:, HD * e : HD * e + HD], gains[0:1, :])
        for s in range(SEQS):
            at = PER_SEQ * s + STEPS * e
            rows[at : at + STEPS, :] = normed[STEPS * s : STEPS * s + STEPS]
    keyval = keyval_part[...]
    high = keyval.astype(BF16).astype(F32)
    rows[64:96, :] = jnp.concatenate([high, keyval - high], axis=1)
    message = rows[...].astype(BF16)
    for i in range(CHIPS):
        out[i] = message


def cached_attention(lengths, mine, theirs, cache, _, out, queries, weighted, scores, weights):
    first = lax.axis_index("tp") * SLOTS
    core = lax.axis_index("tp") % 2
    for i in range(CHIPS):
        queries[2 * i + core] = mine[i, 0:64, :].astype(F32)
        queries[2 * i + 1 - core] = theirs[i, 0:64, :].astype(F32)
    position = lanes((HD, SLOTS)) + first
    lane = lanes((HD, HD))
    for s in range(SEQS):
        query = queries[:, PER_SEQ * s : PER_SEQ * s + PER_SEQ, :].reshape(HD, HD).astype(BF16)
        for c in range(KVH):
            scores[s, ROWS * c : ROWS * c + ROWS, :] = lax.dot_general(
                query[ROWS * c : ROWS * c + ROWS],
                cache[0, s, 0, c],
                NT,
                preferred_element_type=F32,
            )
    logs = jnp.zeros((HD, HD), F32)
    inverse = []
    for s in range(SEQS):
        score = jnp.where(position < lengths[0, s], scores[s] * INV_ROOT, FAR)
        largest = score.max(axis=-1, keepdims=True)
        weight = jnp.exp(score - largest)
        total = weight.sum(axis=-1, keepdims=True)
        weights[s] = weight.astype(BF16)
        log = jnp.where(largest > 0.5 * FAR, largest + jnp.log(total), FAR)
        logs = jnp.where(lane % SEQS == s, log, logs)
        inverse.append(1.0 / total)
    for s in range(SEQS):
        value = [
            jnp.dot(
                weights[s, ROWS * c : ROWS * c + ROWS, :],
                cache[0, s, 1, c],
                preferred_element_type=F32,
            )
            for c in range(KVH)
        ]
        value = jnp.concatenate(value, axis=0) * inverse[s]
        weighted[:, PER_SEQ * s : PER_SEQ * s + PER_SEQ, :] = value.reshape(TP, PER_SEQ, HD)
    high = logs.astype(BF16).astype(F32)
    middle = (logs - high).astype(BF16).astype(F32)
    terms = jnp.where(lane < 8, high, jnp.where(lane < 16, middle, logs - high - middle))
    weighted[:, 64:72, :] = terms.reshape(TP, PER_SEQ, HD)
    weighted[:, 72:80, :] = jnp.zeros((TP, 8, HD), F32)
    for i in range(TP):
        out[i] = weighted[i].astype(BF16)


def fresh_attention(mine, theirs, gains, out, logs):
    me = lax.axis_index("tp")
    even = me % 2 == 0
    head = me // (TP // KVH)
    lane = lanes((ROWS, HD))

    def raw(chip):
        own = mine[chip, 64:96, :].astype(F32)
        own = own + pltpu.roll(own, R, 1)
        other = theirs[chip, 64:96, :].astype(F32)
        other = other + pltpu.roll(other, R, 1)
        return jnp.where((lane < R) == even, own, other)

    keys = norm(raw(head), gains[1:2, :]).astype(BF16)
    values = raw(KVH + head).astype(BF16)
    scores = (
        lax.dot_general(mine[me // 2, 0:64, :], keys, NT, preferred_element_type=F32) * INV_ROOT
    )
    row = lax.broadcasted_iota(jnp.int32, (64, ROWS), 0)
    column = lanes((64, ROWS))
    seen = (row // PER_SEQ == column // STEPS) & (row % STEPS >= column % STEPS)
    scores = jnp.where(seen, scores, FAR)
    largest = scores.max(axis=-1, keepdims=True)
    weights = jnp.where(seen, jnp.exp(scores - largest), 0.0)
    total = weights.sum(axis=-1, keepdims=True)
    value = jnp.dot(weights.astype(BF16), values, preferred_element_type=F32)
    out[...] = value / total
    log = largest + jnp.log(total)
    lane = lanes((PER_SEQ, HD))
    compact = jnp.zeros((PER_SEQ, HD), F32)
    for s in range(SEQS):
        compact = jnp.where(lane == s, log[PER_SEQ * s : PER_SEQ * s + PER_SEQ], compact)
    logs[...] = compact


def project(received, fresh, fresh_logs, ao, o_weight, mine, theirs, attended, o_in, sem):
    copy = pltpu.make_async_copy(o_weight, o_in, sem)
    copy.start()
    logs = []
    for i in range(TP):
        terms = received[i, 64:80, :].astype(F32)[0:8]
        logs.append(terms + pltpu.roll(terms, HD - 8, 1) + pltpu.roll(terms, HD - 16, 1))
    logs.append(fresh_logs[...])
    largest = functools.reduce(jnp.maximum, logs)
    shares = [jnp.exp(log - largest) for log in logs]
    inverse = 1.0 / functools.reduce(jnp.add, shares)
    shares = [share * inverse for share in shares]
    for pair in range(SEQS // 2):
        blocks = [received[i, 16 * pair : 16 * pair + 16, :].astype(F32) for i in range(TP)]
        for s in (2 * pair, 2 * pair + 1):
            at = PER_SEQ * s
            total = fresh[at : at + PER_SEQ, :] * shares[TP][:, s : s + 1]
            for i in range(TP):
                part = blocks[i][at - 16 * pair : at - 16 * pair + PER_SEQ]
                total = total + part * shares[i][:, s : s + 1]
            for e in range(2):
                attended[STEPS * s : STEPS * s + STEPS, HD * e : HD * e + HD] = total[
                    STEPS * e : STEPS * e + STEPS
                ]
    heads = attended[...].astype(BF16)
    copy.wait()
    low = lax.dot_general(heads, ao[...], NT, preferred_element_type=F32)
    lane = lanes((ROWS, HD))
    even = lax.axis_index("tp") % 2 == 0
    for k in range(CHIPS):
        at = 2 * OUT * k
        value = jnp.dot(heads, o_in[:, at : at + 2 * OUT], preferred_element_type=F32)
        middle = value[:, 2 * HD : 3 * HD]
        first = [value[:, 0:HD], value[:, HD : 2 * HD], jnp.where(lane < R, middle, low)]
        second = [jnp.where(lane < R, low, middle), value[:, 3 * HD : 4 * HD], value[:, 4 * HD :]]
        for part in range(3):
            at = HD * part
            mine[k, :, at : at + HD] = jnp.where(even, first[part], second[part])
            theirs[k, :, at : at + HD] = jnp.where(even, second[part], first[part]).astype(BF16)


def add_pair(mine, theirs, out):
    for k in range(CHIPS):
        out[k] = (mine[k] + theirs[k].astype(F32)).astype(BF16)


def finish(received, bo, out):
    odd = lax.axis_index("tp") % 2 == 1
    total = received[0].astype(F32)
    for i in range(1, CHIPS):
        total = total + received[i].astype(F32)
    lane = lanes((ROWS, HD))
    low = jnp.where(
        odd,
        jnp.where(lane < R, total[:, :HD], 0.0),
        jnp.where(lane < R, 0.0, total[:, 2 * HD :]),
    )
    high = low.astype(BF16)
    rest = (low - high.astype(F32)).astype(BF16)
    extra = jnp.dot(high, bo[...], preferred_element_type=F32) + jnp.dot(
        rest, bo[...], preferred_element_type=F32
    )
    moved = pltpu.roll(total, 3 * HD - R, 1)
    result = (jnp.where(odd, moved, total) + 0.5 * extra)[:, :OUT].astype(BF16)
    for s in range(SEQS):
        out[0, s] = result[STEPS * s : STEPS * s + STEPS]


def call(kernel, in_specs, outs, scratch=(), vmem=24):
    single = not isinstance(outs, (list, tuple))
    return pl.pallas_call(
        kernel,
        out_shape=outs,
        in_specs=in_specs,
        out_specs=VMEM if single else [VMEM] * len(outs),
        scratch_shapes=list(scratch),
        cost_estimate=pl.CostEstimate(flops=1_000_000, bytes_accessed=1_000_000, transcendentals=0),
        compiler_params=pltpu.CompilerParams(vmem_limit_bytes=vmem * 1024 * 1024),
    )


def shape(*dims, dtype=BF16):
    return jax.ShapeDtypeStruct(dims, dtype)


def per_device(
    hidden_in,
    q_weight,
    kv_weight,
    o_weight,
    q_gain,
    k_gain,
    cache,
    lengths,
    owner,
    a_q,
    b_q,
    a_o,
    b_o,
):
    tokens = hidden_in.reshape(ROWS, WIDTH)
    other_core = [(i, i ^ 1) for i in range(TP)]
    same_core = [list(range(0, TP, 2)), list(range(1, TP, 2))]
    q_gain, k_gain = q_gain.reshape(1, HD), k_gain.reshape(1, HD)

    message = call(
        pack_factors,
        [HBM] * 4,
        shape(GROUPS, FACTOR_ROWS, HD),
        [
            pltpu.VMEM((R, BLOCK), BF16),
            pltpu.VMEM((4, 2 * HD), BF16),
            pltpu.VMEM((4, 2 * HD), BF16),
            pltpu.VMEM((4, OUT), BF16),
            pltpu.VMEM((BLOCK, HD), F32),
            pltpu.VMEM((FACTOR_ROWS, HD), F32),
            pltpu.SemaphoreType.DMA((4,)),
        ],
        vmem=60,
    )(a_q.T, b_q, a_o.T, b_o)
    factors = lax.all_to_all(message, "group", 0, 0)

    query_part = jnp.dot(tokens, q_weight, preferred_element_type=F32)
    keyval_part = jnp.dot(tokens, kv_weight, preferred_element_type=F32)

    gains = jnp.concatenate([q_gain, k_gain], axis=0)
    low_own = call(
        low_rank,
        [SMEM, VMEM, VMEM, VMEM, VMEM],
        shape(ROWS, HD, dtype=F32),
        [pltpu.VMEM((WIDTH, HD), BF16)],
    )(owner, tokens, factors, keyval_part, gains)
    low_other = lax.ppermute(low_own, "tp", other_core)
    bq, ao, bo = call(
        unpack_factors,
        [VMEM],
        [shape(2 * R, 2 * HD), shape(2 * R, 2 * HD), shape(2 * R, 3 * HD)],
        [pltpu.VMEM((R, 3 * HD), F32)],
    )(factors)
    message = call(
        pack_queries,
        [VMEM] * 6,
        shape(CHIPS, QKV_ROWS, HD),
        [pltpu.VMEM((QKV_ROWS, HD), F32)],
    )(query_part, keyval_part, low_own, low_other, bq, gains)
    mine = lax.all_to_all(message, "tp", 0, 0, axis_index_groups=same_core)
    cache = call(
        stage_cache,
        [ANY, ANY],
        shape(*cache.shape),
        [pltpu.SemaphoreType.DMA((SEQS,))],
    )(cache, message)
    theirs = lax.ppermute(mine, "tp", other_core)

    fresh, fresh_logs = call(
        fresh_attention,
        [VMEM] * 3,
        [shape(64, HD, dtype=F32), shape(PER_SEQ, HD, dtype=F32)],
    )(mine, theirs, gains)

    message = call(
        cached_attention,
        [SMEM, VMEM, VMEM, VMEM, VMEM],
        shape(TP, PART_ROWS, HD),
        [
            pltpu.VMEM((TP, 64, HD), F32),
            pltpu.VMEM((TP, PART_ROWS, HD), F32),
            pltpu.VMEM((SEQS, HD, SLOTS), F32),
            pltpu.VMEM((SEQS, HD, SLOTS), BF16),
        ],
    )(lengths, mine, theirs, cache, fresh_logs)
    parts = lax.all_to_all(message, "tp", 0, 0)
    mine, theirs = call(
        project,
        [VMEM] * 4 + [ANY],
        [shape(CHIPS, ROWS, 3 * HD, dtype=F32), shape(CHIPS, ROWS, 3 * HD)],
        [
            pltpu.VMEM((ROWS, 2 * HD), F32),
            pltpu.VMEM((2 * HD, WIDTH), BF16),
            pltpu.SemaphoreType.DMA(()),
        ],
    )(parts, fresh, fresh_logs, ao, o_weight)
    theirs = lax.ppermute(theirs, "tp", other_core)
    message = call(add_pair, [VMEM, VMEM], shape(CHIPS, ROWS, 3 * HD))(mine, theirs)
    sums = lax.all_to_all(message, "tp", 0, 0, axis_index_groups=same_core)
    return call(finish, [VMEM, VMEM], shape(1, SEQS, STEPS, OUT))(sums, bo)


def solution(mesh):
    placed = (
        P("group", None, None, None),
        P(None, "tp"),
        P(None, "tp"),
        P("tp", None),
        P(),
        P(),
        P("group", None, None, None, "tp", None),
        P("group", None),
        P(),
        P("group", None),
        P("group", "tp"),
        P("tp", "group"),
        P("group", "tp"),
    )
    return jax.shard_map(
        per_device,
        mesh=mesh,
        in_specs=placed,
        out_specs=P("group", None, None, "tp"),
        check_vma=False,
    )
```

```python
import functools
import math

import jax
import jax.numpy as jnp
from jax import lax
from jax.experimental import pallas as pl
from jax.experimental.pallas import tpu as pltpu
from jax.sharding import PartitionSpec as P

HD = 128
QH = 32
KVH = 4
R = 64
TP = 16
CHIPS = TP // 2
GROUPS = 16
SEQS = 8
STEPS = 4
ROWS = SEQS * STEPS
PER_SEQ = 2 * STEPS
WIDTH = 5120
SLOTS = 256
BLOCK = WIDTH // GROUPS
HALF = BLOCK // 2
OUT = WIDTH // TP
INV_ROOT = 1.0 / math.sqrt(HD)
FAR = -1e30
BF16 = jnp.bfloat16
F32 = jnp.float32

BQ_AT = 80
AO_AT = 88
BO_AT = 96
FACTOR_ROWS = 112
QKV_ROWS = 80
PART_ROWS = 80

VMEM = pl.BlockSpec(memory_space=pltpu.VMEM)
HBM = pl.BlockSpec(memory_space=pltpu.HBM)
ANY = pl.BlockSpec(memory_space=pl.ANY)
SMEM = pl.BlockSpec(memory_space=pltpu.SMEM)
NT = (((1,), (1,)), ((), ()))


def lanes(shape):
    return lax.broadcasted_iota(jnp.int32, shape, len(shape) - 1)


def norm(values, gain):
    mean_square = jnp.mean(values * values, axis=-1, keepdims=True)
    return values * lax.rsqrt(mean_square + 1e-06) * gain


def pack_factors(a_q, b_q, a_o, b_o, out, a_q_in, b_q_in, a_o_in, b_o_in, turned, rows, sems):
    pairs = ((a_q, a_q_in), (b_q, b_q_in), (a_o, a_o_in), (b_o, b_o_in))
    copies = [
        pltpu.make_async_copy(source, place, sems.at[k]) for k, (source, place) in enumerate(pairs)
    ]
    for copy in copies:
        copy.start()
    for copy in copies:
        copy.wait()
    row = lax.broadcasted_iota(jnp.int32, (R, HD), 0)
    unit = jnp.where(lanes((R, HD)) % R == row, 1.0, 0.0).astype(BF16)
    turned[...] = lax.dot_general(
        a_q_in[...], unit, (((0,), (0,)), ((), ())), preferred_element_type=F32
    )
    start = pl.multiple_of((lax.axis_index("tp") % 2) * HALF, HALF)
    first = turned[pl.ds(start, 80), :]
    second = turned[pl.ds(start + 80, 80), :]
    rows[0:80, :] = jnp.where(lanes((80, HD)) < R, first, second)
    bq = b_q_in[...].astype(F32)
    rows[BQ_AT : BQ_AT + 4, :] = bq[:, :HD]
    rows[BQ_AT + 4 : BQ_AT + 8, :] = bq[:, HD:]
    ao = a_o_in[...].astype(F32)
    rows[AO_AT : AO_AT + 4, :] = ao[:, :HD]
    rows[AO_AT + 4 : AO_AT + 8, :] = ao[:, HD:]
    bo = b_o_in[...].astype(F32)
    rows[BO_AT : BO_AT + 4, :] = bo[:, :HD]
    rows[BO_AT + 4 : BO_AT + 8, :] = bo[:, HD : 2 * HD]
    rows[BO_AT + 8 : BO_AT + 16, :] = jnp.zeros((8, HD), F32)
    rows[BO_AT + 8 : BO_AT + 12, 0:64] = bo[:, 2 * HD :]
    message = rows[...].astype(BF16)
    for g in range(GROUPS):
        out[g] = message


def stage_cache(cache, _, out, sems):
    copies = [pltpu.make_async_copy(cache.at[0, s], out.at[0, s], sems.at[s]) for s in range(SEQS)]
    for copy in copies:
        copy.start()
    for copy in copies:
        copy.wait()


def low_rank(owner, tokens, factors, _, __, out, a_true):
    core = lax.axis_index("tp") % 2
    lane = lanes((80, HD))
    left = jnp.where(lane < R, 1.0, 0.0).astype(BF16)
    right = jnp.where(lane < R, 0.0, 1.0).astype(BF16)
    empty = jnp.zeros((HALF, HD), BF16)
    for g in range(GROUPS):
        base = owner[g] * BLOCK
        mine = pl.multiple_of(base + core * HALF, 32)
        other = pl.multiple_of(base + (1 - core) * HALF, 32)
        block = factors[g, 0:80, :]
        a_true[pl.ds(mine, 80), :] = block * left
        a_true[pl.ds(pl.multiple_of(mine + 80, 16), 80), :] = block * right
        a_true[pl.ds(other, HALF), :] = empty
    both = jnp.dot(tokens[...], a_true[...], preferred_element_type=F32)
    out[...] = both + pltpu.roll(both, R, 1)


def unpack_factors(factors, bq_out, ao_out, bo_out, rows):
    for at, pieces, out in ((BQ_AT, 2, bq_out), (AO_AT, 2, ao_out), (BO_AT, 3, bo_out)):
        for g in range(GROUPS):
            block = factors[g, BQ_AT:FACTOR_ROWS, :].astype(F32)
            for h in range(pieces):
                piece = block[at - BQ_AT + 4 * h : at - BQ_AT + 4 * h + 4]
                rows[4 * g : 4 * g + 4, HD * h : HD * h + HD] = piece
        whole = rows[:, : HD * pieces].astype(BF16)
        out[0:R, :] = whole
        out[R : 2 * R, :] = whole


def pack_queries(query_part, kv_own, kv_other, low_own, low_other, bq, gains, out, rows):
    chip, core = lax.axis_index("tp") // 2, lax.axis_index("tp") % 2
    low = low_own[...] + low_other[...]
    lane = lanes((ROWS, HD))
    high = low.astype(BF16).astype(F32)
    low_terms = jnp.where(lane < R, high, low - high).astype(BF16)
    query = query_part[...] + 0.5 * jnp.dot(low_terms, bq[...], preferred_element_type=F32)
    for e in range(2):
        normed = norm(query[:, HD * e : HD * e + HD], gains[0:1, :])
        for s in range(SEQS):
            at = PER_SEQ * s + STEPS * e
            rows[at : at + STEPS, :] = normed[STEPS * s : STEPS * s + STEPS]
    own, other = kv_own[...], kv_other[...]
    left, right = jnp.where(core == 0, own, other), jnp.where(core == 0, other, own)
    head = jnp.concatenate([left, right], axis=1)
    head = jnp.where(chip < KVH, norm(head, gains[1:2, :]), head)
    rows[64:80, :] = jnp.where(core == 0, head[0:16], head[16:32])
    message = rows[...].astype(BF16)
    for i in range(CHIPS):
        out[i] = message


def cached_attention(
    lengths, mine, theirs, cache, own_part, other_part, queries, weighted, scores, weights
):
    first = lax.axis_index("tp") * SLOTS
    core = lax.axis_index("tp") % 2
    for i in range(CHIPS):
        queries[2 * i + core] = mine[i, 0:64, :].astype(F32)
        queries[2 * i + 1 - core] = theirs[i, 0:64, :].astype(F32)
    position = lanes((HD, SLOTS)) + first
    lane = lanes((HD, HD))
    for s in range(SEQS):
        query = queries[:, PER_SEQ * s : PER_SEQ * s + PER_SEQ, :].reshape(HD, HD).astype(BF16)
        for c in range(KVH):
            scores[s, ROWS * c : ROWS * c + ROWS, :] = lax.dot_general(
                query[ROWS * c : ROWS * c + ROWS],
                cache[0, s, 0, c],
                NT,
                preferred_element_type=F32,
            )
    logs = jnp.zeros((HD, HD), F32)
    inverse = []
    for s in range(SEQS):
        score = jnp.where(position < lengths[0, s], scores[s] * INV_ROOT, FAR)
        largest = score.max(axis=-1, keepdims=True)
        weight = jnp.exp(score - largest)
        total = weight.sum(axis=-1, keepdims=True)
        weights[s] = weight.astype(BF16)
        log = jnp.where(largest > 0.5 * FAR, largest + jnp.log(total), FAR)
        logs = jnp.where(lane % SEQS == s, log, logs)
        inverse.append(1.0 / total)
    for s in range(SEQS):
        value = [
            jnp.dot(
                weights[s, ROWS * c : ROWS * c + ROWS, :],
                cache[0, s, 1, c],
                preferred_element_type=F32,
            )
            for c in range(KVH)
        ]
        value = jnp.concatenate(value, axis=0) * inverse[s]
        weighted[:, PER_SEQ * s : PER_SEQ * s + PER_SEQ, :] = value.reshape(TP, PER_SEQ, HD)
    high = logs.astype(BF16).astype(F32)
    middle = (logs - high).astype(BF16).astype(F32)
    terms = jnp.where(lane < 8, high, jnp.where(lane < 16, middle, logs - high - middle))
    weighted[:, 64:72, :] = terms.reshape(TP, PER_SEQ, HD)
    weighted[:, 72:80, :] = jnp.zeros((TP, 8, HD), F32)
    for i in range(CHIPS):
        own_part[i] = weighted[2 * i + core]
        other_part[i] = weighted[2 * i + 1 - core].astype(BF16)


def log_sum(terms):
    return terms + pltpu.roll(terms, HD - 8, 1) + pltpu.roll(terms, HD - 16, 1)


def spread(shares):
    rows = shares.shape[0]
    high = shares.astype(BF16).astype(F32)
    low = pltpu.roll(shares - high, SEQS, 1)
    terms = jnp.where(lanes((rows, HD)) < SEQS, high, low).astype(BF16)[:, : 2 * SEQS]
    row = lax.broadcasted_iota(jnp.int32, (2 * SEQS, SEQS * HD), 0)
    unit = jnp.where(row % SEQS == lanes((2 * SEQS, SEQS * HD)) // HD, 1.0, 0.0).astype(BF16)
    return jnp.dot(terms, unit, preferred_element_type=F32)


def merge_parts(own, other, _, out):
    lane = lanes((64, HD))
    theirs = [other[i].astype(F32) for i in range(CHIPS)]
    logs = [
        log_sum(jnp.concatenate([own[i, 64:72, :] for i in range(CHIPS)], axis=0)),
        log_sum(jnp.concatenate([part[64:72] for part in theirs], axis=0)),
    ]
    largest = jnp.maximum(logs[0], logs[1])
    shares = [jnp.exp(log - largest) for log in logs]
    total = shares[0] + shares[1]
    inverse = 1.0 / total
    wide = spread(jnp.concatenate([shares[0] * inverse, shares[1] * inverse], axis=0))
    log = largest + jnp.log(total)
    high = log.astype(BF16).astype(F32)
    middle = (log - high).astype(BF16).astype(F32)
    low = log - high - middle
    terms = jnp.where(lane < 16, pltpu.roll(middle, 8, 1), pltpu.roll(low, 16, 1))
    terms = jnp.where(lane < 8, high, terms)
    for i in range(CHIPS):
        at = PER_SEQ * i
        rows = []
        for s in range(SEQS):
            block = slice(HD * s, HD * s + HD)
            rows.append(
                own[i, PER_SEQ * s : PER_SEQ * s + PER_SEQ, :] * wide[at : at + PER_SEQ, block]
                + theirs[i][PER_SEQ * s : PER_SEQ * s + PER_SEQ]
                * wide[64 + at : 64 + at + PER_SEQ, block]
            )
        rows.append(terms[at : at + PER_SEQ])
        rows.append(jnp.zeros((PER_SEQ, HD), F32))
        out[i] = jnp.concatenate(rows, axis=0).astype(BF16)


def fresh_attention(mine, theirs, out, logs):
    chip, core = lax.axis_index("tp") // 2, lax.axis_index("tp") % 2
    head = chip // (CHIPS // KVH)

    def whole(at):
        own, other = mine[at, 64:80, :].astype(F32), theirs[at, 64:80, :].astype(F32)
        low, high = jnp.where(core == 0, own, other), jnp.where(core == 0, other, own)
        return jnp.concatenate([low, high], axis=0).astype(BF16)

    keys, values = whole(head), whole(KVH + head)
    scores = (
        lax.dot_general(mine[chip, 0:64, :], keys, NT, preferred_element_type=F32) * INV_ROOT
    )
    row = lax.broadcasted_iota(jnp.int32, (64, ROWS), 0)
    column = lanes((64, ROWS))
    seen = (row // PER_SEQ == column // STEPS) & (row % STEPS >= column % STEPS)
    scores = jnp.where(seen, scores, FAR)
    largest = scores.max(axis=-1, keepdims=True)
    weights = jnp.where(seen, jnp.exp(scores - largest), 0.0)
    total = weights.sum(axis=-1, keepdims=True)
    value = jnp.dot(weights.astype(BF16), values, preferred_element_type=F32)
    out[...] = value / total
    log = largest + jnp.log(total)
    lane = lanes((PER_SEQ, HD))
    compact = jnp.zeros((PER_SEQ, HD), F32)
    for s in range(SEQS):
        compact = jnp.where(lane == s, log[PER_SEQ * s : PER_SEQ * s + PER_SEQ], compact)
    logs[...] = compact


def place_columns(heads, low, o_in, core, out):
    lane = lanes((ROWS, HD))
    for k in range(CHIPS):
        start = pl.multiple_of(2 * OUT * k + 2 * HD * core, HD)
        value = jnp.dot(heads, o_in[:, pl.ds(start, 3 * HD)], preferred_element_type=F32)
        first, last = value[:, :HD], value[:, 2 * HD :]
        first = jnp.where((lane < R) & (core == 1), low, first)
        last = jnp.where((lane >= R) & (core == 0), low, last)
        out[k, :, 0:HD] = first.astype(out.dtype)
        out[k, :, HD : 2 * HD] = value[:, HD : 2 * HD].astype(out.dtype)
        out[k, :, 2 * HD :] = last.astype(out.dtype)


def project_theirs(
    received, fresh, fresh_logs, ao, o_in, theirs, heads, low, attended
):
    logs = []
    for i in range(CHIPS):
        logs.append(log_sum(received[i, 64:80, :].astype(F32)[0:8]))
    logs.append(fresh_logs[...])
    largest = functools.reduce(jnp.maximum, logs)
    shares = [jnp.exp(log - largest) for log in logs]
    inverse = 1.0 / functools.reduce(jnp.add, shares)
    wide = spread(jnp.concatenate([share * inverse for share in shares], axis=0))
    for pair in range(SEQS // 2):
        blocks = [received[i, 16 * pair : 16 * pair + 16, :].astype(F32) for i in range(CHIPS)]
        for s in (2 * pair, 2 * pair + 1):
            at, block = PER_SEQ * s, slice(HD * s, HD * s + HD)
            total = fresh[at : at + PER_SEQ, :] * wide[64:72, block]
            for i in range(CHIPS):
                part = blocks[i][at - 16 * pair : at - 16 * pair + PER_SEQ]
                total = total + part * wide[PER_SEQ * i : PER_SEQ * i + PER_SEQ, block]
            for e in range(2):
                attended[STEPS * s : STEPS * s + STEPS, HD * e : HD * e + HD] = total[
                    STEPS * e : STEPS * e + STEPS
                ]
    heads[...] = attended[...].astype(BF16)
    low[...] = lax.dot_general(heads[...], ao[...], NT, preferred_element_type=F32)
    place_columns(heads[...], low[...], o_in, 1 - lax.axis_index("tp") % 2, theirs)


def project_mine(heads, low, o_in, mine):
    place_columns(heads[...], low[...], o_in, lax.axis_index("tp") % 2, mine)


def add_pair(mine, theirs, out):
    for k in range(CHIPS):
        out[k] = (mine[k] + theirs[k].astype(F32)).astype(BF16)


def finish(received, bo, out):
    odd = lax.axis_index("tp") % 2 == 1
    total = received[0].astype(F32)
    for i in range(1, CHIPS):
        total = total + received[i].astype(F32)
    lane = lanes((ROWS, HD))
    low = jnp.where(
        odd,
        jnp.where(lane < R, total[:, :HD], 0.0),
        jnp.where(lane < R, 0.0, total[:, 2 * HD :]),
    )
    high = low.astype(BF16)
    rest = (low - high.astype(F32)).astype(BF16)
    extra = jnp.dot(high, bo[...], preferred_element_type=F32) + jnp.dot(
        rest, bo[...], preferred_element_type=F32
    )
    moved = pltpu.roll(total, 3 * HD - R, 1)
    result = (jnp.where(odd, moved, total) + 0.5 * extra)[:, :OUT].astype(BF16)
    for s in range(SEQS):
        out[0, s] = result[STEPS * s : STEPS * s + STEPS]


def call(kernel, in_specs, outs, scratch=(), vmem=24):
    single = not isinstance(outs, (list, tuple))
    return pl.pallas_call(
        kernel,
        out_shape=outs,
        in_specs=in_specs,
        out_specs=VMEM if single else [VMEM] * len(outs),
        scratch_shapes=list(scratch),
        cost_estimate=pl.CostEstimate(flops=1_000_000, bytes_accessed=1_000_000, transcendentals=0),
        compiler_params=pltpu.CompilerParams(vmem_limit_bytes=vmem * 1024 * 1024),
    )


def shape(*dims, dtype=BF16):
    return jax.ShapeDtypeStruct(dims, dtype)


def per_device(
    hidden_in,
    q_weight,
    kv_weight,
    o_weight,
    q_gain,
    k_gain,
    cache,
    lengths,
    owner,
    a_q,
    b_q,
    a_o,
    b_o,
):
    tokens = hidden_in.reshape(ROWS, WIDTH)
    other_core = [(i, i ^ 1) for i in range(TP)]
    same_core = [list(range(0, TP, 2)), list(range(1, TP, 2))]
    q_gain, k_gain = q_gain.reshape(1, HD), k_gain.reshape(1, HD)

    message = call(
        pack_factors,
        [HBM] * 4,
        shape(GROUPS, FACTOR_ROWS, HD),
        [
            pltpu.VMEM((R, BLOCK), BF16),
            pltpu.VMEM((4, 2 * HD), BF16),
            pltpu.VMEM((4, 2 * HD), BF16),
            pltpu.VMEM((4, OUT), BF16),
            pltpu.VMEM((BLOCK, HD), F32),
            pltpu.VMEM((FACTOR_ROWS, HD), F32),
            pltpu.SemaphoreType.DMA((4,)),
        ],
        vmem=60,
    )(a_q.T, b_q, a_o.T, b_o)
    factors = lax.all_to_all(message, "group", 0, 0)

    query_part = jnp.dot(tokens, q_weight, preferred_element_type=F32)
    keyval_part = jnp.dot(tokens, kv_weight, preferred_element_type=F32)

    gains = jnp.concatenate([q_gain, k_gain], axis=0)
    kv_other = lax.ppermute(keyval_part, "tp", other_core)
    low_own = call(
        low_rank,
        [SMEM, VMEM, VMEM, VMEM, VMEM],
        shape(ROWS, HD, dtype=F32),
        [pltpu.VMEM((WIDTH, HD), BF16)],
    )(owner, tokens, factors, kv_other, gains)
    low_other = lax.ppermute(low_own, "tp", other_core)
    bq, ao, bo = call(
        unpack_factors,
        [VMEM],
        [shape(2 * R, 2 * HD), shape(2 * R, 2 * HD), shape(2 * R, 3 * HD)],
        [pltpu.VMEM((R, 3 * HD), F32)],
    )(factors)
    message = call(
        pack_queries,
        [VMEM] * 7,
        shape(CHIPS, QKV_ROWS, HD),
        [pltpu.VMEM((QKV_ROWS, HD), F32)],
    )(query_part, keyval_part, kv_other, low_own, low_other, bq, gains)
    mine = lax.all_to_all(message, "tp", 0, 0, axis_index_groups=same_core)
    cache = call(
        stage_cache,
        [ANY, ANY],
        shape(*cache.shape),
        [pltpu.SemaphoreType.DMA((SEQS,))],
    )(cache, message)
    theirs = lax.ppermute(mine, "tp", other_core)

    own_part, other_part = call(
        cached_attention,
        [SMEM, VMEM, VMEM, VMEM],
        [shape(CHIPS, PART_ROWS, HD, dtype=F32), shape(CHIPS, PART_ROWS, HD)],
        [
            pltpu.VMEM((TP, 64, HD), F32),
            pltpu.VMEM((TP, PART_ROWS, HD), F32),
            pltpu.VMEM((SEQS, HD, SLOTS), F32),
            pltpu.VMEM((SEQS, HD, SLOTS), BF16),
        ],
    )(lengths, mine, theirs, cache)
    other_part = lax.ppermute(other_part, "tp", other_core)
    fresh, fresh_logs = call(
        fresh_attention,
        [VMEM] * 2,
        [shape(64, HD, dtype=F32), shape(PER_SEQ, HD, dtype=F32)],
    )(mine, theirs)

    message = call(merge_parts, [VMEM] * 3, shape(CHIPS, PART_ROWS, HD))(
        own_part, other_part, fresh_logs
    )
    parts = lax.all_to_all(message, "tp", 0, 0, axis_index_groups=same_core)
    theirs, heads, low = call(
        project_theirs,
        [VMEM] * 5,
        [shape(CHIPS, ROWS, 3 * HD), shape(ROWS, 2 * HD), shape(ROWS, HD, dtype=F32)],
        [pltpu.VMEM((ROWS, 2 * HD), F32)],
    )(parts, fresh, fresh_logs, ao, o_weight)
    theirs = lax.ppermute(theirs, "tp", other_core)
    mine = call(
        project_mine,
        [VMEM] * 3,
        shape(CHIPS, ROWS, 3 * HD, dtype=F32),
    )(heads, low, o_weight)
    message = call(add_pair, [VMEM, VMEM], shape(CHIPS, ROWS, 3 * HD))(mine, theirs)
    sums = lax.all_to_all(message, "tp", 0, 0, axis_index_groups=same_core)
    return call(finish, [VMEM, VMEM], shape(1, SEQS, STEPS, OUT))(sums, bo)


def solution(mesh):
    placed = (
        P("group", None, None, None),
        P(None, "tp"),
        P(None, "tp"),
        P("tp", None),
        P(),
        P(),
        P("group", None, None, None, "tp", None),
        P("group", None),
        P(),
        P("group", None),
        P("group", "tp"),
        P("tp", "group"),
        P("group", "tp"),
    )
    return jax.shard_map(
        per_device,
        mesh=mesh,
        in_specs=placed,
        out_specs=P("group", None, None, "tp"),
        check_vma=False,
    )
```

```python
import functools
import math

import jax
import jax.numpy as jnp
from jax import lax
from jax.experimental import pallas as pl
from jax.experimental.pallas import tpu as pltpu
from jax.sharding import PartitionSpec as P

HD = 128
QH = 32
KVH = 4
R = 64
TP = 16
CHIPS = TP // 2
GROUPS = 16
SEQS = 8
STEPS = 4
ROWS = SEQS * STEPS
PER_SEQ = 2 * STEPS
WIDTH = 5120
SLOTS = 256
BLOCK = WIDTH // GROUPS
HALF = BLOCK // 2
OUT = WIDTH // TP
INV_ROOT = 1.0 / math.sqrt(HD)
FAR = -1e30
BF16 = jnp.bfloat16
F32 = jnp.float32

BQ_AT = 80
AO_AT = 88
BO_AT = 96
FACTOR_ROWS = 112
QKV_ROWS = 80
PART_ROWS = 80

VMEM = pl.BlockSpec(memory_space=pltpu.VMEM)
HBM = pl.BlockSpec(memory_space=pltpu.HBM)
ANY = pl.BlockSpec(memory_space=pl.ANY)
SMEM = pl.BlockSpec(memory_space=pltpu.SMEM)
NT = (((1,), (1,)), ((), ()))


def lanes(shape):
    return lax.broadcasted_iota(jnp.int32, shape, len(shape) - 1)


def norm(values, gain):
    mean_square = jnp.mean(values * values, axis=-1, keepdims=True)
    return values * lax.rsqrt(mean_square + 1e-06) * gain


def pack_factors(a_q, b_q, a_o, b_o, out, a_q_in, b_q_in, a_o_in, b_o_in, turned, rows, sems):
    pairs = ((a_q, a_q_in), (b_q, b_q_in), (a_o, a_o_in), (b_o, b_o_in))
    copies = [
        pltpu.make_async_copy(source, place, sems.at[k]) for k, (source, place) in enumerate(pairs)
    ]
    for copy in copies:
        copy.start()
    for copy in copies:
        copy.wait()
    row = lax.broadcasted_iota(jnp.int32, (R, HD), 0)
    unit = jnp.where(lanes((R, HD)) % R == row, 1.0, 0.0).astype(BF16)
    turned[...] = lax.dot_general(
        a_q_in[...], unit, (((0,), (0,)), ((), ())), preferred_element_type=F32
    )
    start = pl.multiple_of((lax.axis_index("tp") % 2) * HALF, HALF)
    first = turned[pl.ds(start, 80), :]
    second = turned[pl.ds(start + 80, 80), :]
    rows[0:80, :] = jnp.where(lanes((80, HD)) < R, first, second)
    bq = b_q_in[...].astype(F32)
    rows[BQ_AT : BQ_AT + 4, :] = bq[:, :HD]
    rows[BQ_AT + 4 : BQ_AT + 8, :] = bq[:, HD:]
    ao = a_o_in[...].astype(F32)
    rows[AO_AT : AO_AT + 4, :] = ao[:, :HD]
    rows[AO_AT + 4 : AO_AT + 8, :] = ao[:, HD:]
    bo = b_o_in[...].astype(F32)
    rows[BO_AT : BO_AT + 4, :] = bo[:, :HD]
    rows[BO_AT + 4 : BO_AT + 8, :] = bo[:, HD : 2 * HD]
    rows[BO_AT + 8 : BO_AT + 16, :] = jnp.zeros((8, HD), F32)
    rows[BO_AT + 8 : BO_AT + 12, 0:64] = bo[:, 2 * HD :]
    message = rows[...].astype(BF16)
    for g in range(GROUPS):
        out[g] = message


def stage_cache(cache, _, out, sems):
    copies = [pltpu.make_async_copy(cache.at[0, s], out.at[0, s], sems.at[s]) for s in range(SEQS)]
    for copy in copies:
        copy.start()
    for copy in copies:
        copy.wait()


def low_rank(owner, tokens, factors, _, __, out, a_true):
    core = lax.axis_index("tp") % 2
    lane = lanes((80, HD))
    left = jnp.where(lane < R, 1.0, 0.0).astype(BF16)
    right = jnp.where(lane < R, 0.0, 1.0).astype(BF16)
    empty = jnp.zeros((HALF, HD), BF16)
    for g in range(GROUPS):
        base = owner[g] * BLOCK
        mine = pl.multiple_of(base + core * HALF, 32)
        other = pl.multiple_of(base + (1 - core) * HALF, 32)
        block = factors[g, 0:80, :]
        a_true[pl.ds(mine, 80), :] = block * left
        a_true[pl.ds(pl.multiple_of(mine + 80, 16), 80), :] = block * right
        a_true[pl.ds(other, HALF), :] = empty
    both = jnp.dot(tokens[...], a_true[...], preferred_element_type=F32)
    out[...] = both + pltpu.roll(both, R, 1)


def unpack_factors(factors, bq_out, ao_out, bo_out, rows):
    for at, pieces, out in ((BQ_AT, 2, bq_out), (AO_AT, 2, ao_out), (BO_AT, 3, bo_out)):
        for g in range(GROUPS):
            block = factors[g, BQ_AT:FACTOR_ROWS, :].astype(F32)
            for h in range(pieces):
                piece = block[at - BQ_AT + 4 * h : at - BQ_AT + 4 * h + 4]
                rows[4 * g : 4 * g + 4, HD * h : HD * h + HD] = piece
        whole = rows[:, : HD * pieces].astype(BF16)
        out[0:R, :] = whole
        out[R : 2 * R, :] = whole


def pack_queries(query_part, kv_own, kv_other, low_own, low_other, bq, gains, out, rows):
    chip, core = lax.axis_index("tp") // 2, lax.axis_index("tp") % 2
    low = low_own[...] + low_other[...]
    lane = lanes((ROWS, HD))
    high = low.astype(BF16).astype(F32)
    low_terms = jnp.where(lane < R, high, low - high).astype(BF16)
    query = query_part[...] + 0.5 * jnp.dot(low_terms, bq[...], preferred_element_type=F32)
    for e in range(2):
        normed = norm(query[:, HD * e : HD * e + HD], gains[0:1, :])
        for s in range(SEQS):
            at = PER_SEQ * s + STEPS * e
            rows[at : at + STEPS, :] = normed[STEPS * s : STEPS * s + STEPS]
    own, other = kv_own[...], kv_other[...]
    left, right = jnp.where(core == 0, own, other), jnp.where(core == 0, other, own)
    head = jnp.concatenate([left, right], axis=1)
    head = jnp.where(chip < KVH, norm(head, gains[1:2, :]), head)
    rows[64:80, :] = jnp.where(core == 0, head[0:16], head[16:32])
    message = rows[...].astype(BF16)
    for i in range(CHIPS):
        out[i] = message


def cached_attention(
    gains, mine, theirs, cache, own_part, other_part, queries, weighted, scores, weights
):
    first = lax.axis_index("tp") * SLOTS
    core = lax.axis_index("tp") % 2
    for i in range(CHIPS):
        queries[2 * i + core] = mine[i, 0:64, :].astype(F32)
        queries[2 * i + 1 - core] = theirs[i, 0:64, :].astype(F32)
    position = (lanes((HD, SLOTS)) + first).astype(F32)
    lane = lanes((HD, HD))
    for s in range(SEQS):
        query = queries[:, PER_SEQ * s : PER_SEQ * s + PER_SEQ, :].reshape(HD, HD).astype(BF16)
        for c in range(KVH):
            scores[s, ROWS * c : ROWS * c + ROWS, :] = lax.dot_general(
                query[ROWS * c : ROWS * c + ROWS],
                cache[0, s, 0, c],
                NT,
                preferred_element_type=F32,
            )
    logs = jnp.zeros((HD, HD), F32)
    inverse = []
    for s in range(SEQS):
        bound = jnp.concatenate([gains[2 + s : 3 + s, :]] * 2, axis=1)
        score = jnp.where(position < bound, scores[s] * INV_ROOT, FAR)
        largest = score.max(axis=-1, keepdims=True)
        weight = jnp.exp(score - largest)
        total = weight.sum(axis=-1, keepdims=True)
        weights[s] = weight.astype(BF16)
        log = jnp.where(largest > 0.5 * FAR, largest + jnp.log(total), FAR)
        logs = jnp.where(lane % SEQS == s, log, logs)
        inverse.append(1.0 / total)
    for s in range(SEQS):
        value = [
            jnp.dot(
                weights[s, ROWS * c : ROWS * c + ROWS, :],
                cache[0, s, 1, c],
                preferred_element_type=F32,
            )
            for c in range(KVH)
        ]
        value = jnp.concatenate(value, axis=0) * inverse[s]
        weighted[:, PER_SEQ * s : PER_SEQ * s + PER_SEQ, :] = value.reshape(TP, PER_SEQ, HD)
    high = logs.astype(BF16).astype(F32)
    middle = (logs - high).astype(BF16).astype(F32)
    terms = jnp.where(lane < 8, high, jnp.where(lane < 16, middle, logs - high - middle))
    weighted[:, 64:72, :] = terms.reshape(TP, PER_SEQ, HD)
    weighted[:, 72:80, :] = jnp.zeros((TP, 8, HD), F32)
    for i in range(CHIPS):
        own_part[i] = weighted[2 * i + core]
        other_part[i] = weighted[2 * i + 1 - core].astype(BF16)


def log_sum(terms):
    return terms + pltpu.roll(terms, HD - 8, 1) + pltpu.roll(terms, HD - 16, 1)


def spread(shares):
    rows = shares.shape[0]
    high = shares.astype(BF16).astype(F32)
    low = pltpu.roll(shares - high, SEQS, 1)
    terms = jnp.where(lanes((rows, HD)) < SEQS, high, low).astype(BF16)[:, : 2 * SEQS]
    row = lax.broadcasted_iota(jnp.int32, (2 * SEQS, SEQS * HD), 0)
    unit = jnp.where(row % SEQS == lanes((2 * SEQS, SEQS * HD)) // HD, 1.0, 0.0).astype(BF16)
    return jnp.dot(terms, unit, preferred_element_type=F32)


def merge_parts(own, other, _, out):
    lane = lanes((64, HD))
    theirs = [other[i].astype(F32) for i in range(CHIPS)]
    logs = [
        log_sum(jnp.concatenate([own[i, 64:72, :] for i in range(CHIPS)], axis=0)),
        log_sum(jnp.concatenate([part[64:72] for part in theirs], axis=0)),
    ]
    largest = jnp.maximum(logs[0], logs[1])
    shares = [jnp.exp(log - largest) for log in logs]
    total = shares[0] + shares[1]
    inverse = 1.0 / total
    wide = spread(jnp.concatenate([shares[0] * inverse, shares[1] * inverse], axis=0))
    log = largest + jnp.log(total)
    high = log.astype(BF16).astype(F32)
    middle = (log - high).astype(BF16).astype(F32)
    low = log - high - middle
    terms = jnp.where(lane < 16, pltpu.roll(middle, 8, 1), pltpu.roll(low, 16, 1))
    terms = jnp.where(lane < 8, high, terms)
    for i in range(CHIPS):
        at = PER_SEQ * i
        rows = []
        for s in range(SEQS):
            block = slice(HD * s, HD * s + HD)
            rows.append(
                own[i, PER_SEQ * s : PER_SEQ * s + PER_SEQ, :] * wide[at : at + PER_SEQ, block]
                + theirs[i][PER_SEQ * s : PER_SEQ * s + PER_SEQ]
                * wide[64 + at : 64 + at + PER_SEQ, block]
            )
        rows.append(terms[at : at + PER_SEQ])
        rows.append(jnp.zeros((PER_SEQ, HD), F32))
        out[i] = jnp.concatenate(rows, axis=0).astype(BF16)


def fresh_attention(mine, theirs, out, logs):
    chip, core = lax.axis_index("tp") // 2, lax.axis_index("tp") % 2
    head = chip // (CHIPS // KVH)

    def whole(at):
        own, other = mine[at, 64:80, :].astype(F32), theirs[at, 64:80, :].astype(F32)
        low, high = jnp.where(core == 0, own, other), jnp.where(core == 0, other, own)
        return jnp.concatenate([low, high], axis=0).astype(BF16)

    keys, values = whole(head), whole(KVH + head)
    scores = (
        lax.dot_general(mine[chip, 0:64, :], keys, NT, preferred_element_type=F32) * INV_ROOT
    )
    row = lax.broadcasted_iota(jnp.int32, (64, ROWS), 0)
    column = lanes((64, ROWS))
    seen = (row // PER_SEQ == column // STEPS) & (row % STEPS >= column % STEPS)
    scores = jnp.where(seen, scores, FAR)
    largest = scores.max(axis=-1, keepdims=True)
    weights = jnp.where(seen, jnp.exp(scores - largest), 0.0)
    total = weights.sum(axis=-1, keepdims=True)
    value = jnp.dot(weights.astype(BF16), values, preferred_element_type=F32)
    out[...] = value / total
    log = largest + jnp.log(total)
    lane = lanes((PER_SEQ, HD))
    compact = jnp.zeros((PER_SEQ, HD), F32)
    for s in range(SEQS):
        compact = jnp.where(lane == s, log[PER_SEQ * s : PER_SEQ * s + PER_SEQ], compact)
    logs[...] = compact


def place_columns(heads, low, o_in, core, out):
    lane = lanes((ROWS, HD))
    for k in range(CHIPS):
        start = pl.multiple_of(2 * OUT * k + 2 * HD * core, HD)
        value = jnp.dot(heads, o_in[:, pl.ds(start, 3 * HD)], preferred_element_type=F32)
        first, last = value[:, :HD], value[:, 2 * HD :]
        first = jnp.where((lane < R) & (core == 1), low, first)
        last = jnp.where((lane >= R) & (core == 0), low, last)
        out[k, :, 0:HD] = first.astype(out.dtype)
        out[k, :, HD : 2 * HD] = value[:, HD : 2 * HD].astype(out.dtype)
        out[k, :, 2 * HD :] = last.astype(out.dtype)


def project_theirs(
    received, fresh, fresh_logs, ao, o_in, theirs, heads, low, attended
):
    logs = []
    for i in range(CHIPS):
        logs.append(log_sum(received[i, 64:80, :].astype(F32)[0:8]))
    logs.append(fresh_logs[...])
    largest = functools.reduce(jnp.maximum, logs)
    shares = [jnp.exp(log - largest) for log in logs]
    inverse = 1.0 / functools.reduce(jnp.add, shares)
    wide = spread(jnp.concatenate([share * inverse for share in shares], axis=0))
    for pair in range(SEQS // 2):
        blocks = [received[i, 16 * pair : 16 * pair + 16, :].astype(F32) for i in range(CHIPS)]
        for s in (2 * pair, 2 * pair + 1):
            at, block = PER_SEQ * s, slice(HD * s, HD * s + HD)
            total = fresh[at : at + PER_SEQ, :] * wide[64:72, block]
            for i in range(CHIPS):
                part = blocks[i][at - 16 * pair : at - 16 * pair + PER_SEQ]
                total = total + part * wide[PER_SEQ * i : PER_SEQ * i + PER_SEQ, block]
            for e in range(2):
                attended[STEPS * s : STEPS * s + STEPS, HD * e : HD * e + HD] = total[
                    STEPS * e : STEPS * e + STEPS
                ]
    heads[...] = attended[...].astype(BF16)
    low[...] = lax.dot_general(heads[...], ao[...], NT, preferred_element_type=F32)
    place_columns(heads[...], low[...], o_in, 1 - lax.axis_index("tp") % 2, theirs)


def project_mine(heads, low, o_in, mine):
    place_columns(heads[...], low[...], o_in, lax.axis_index("tp") % 2, mine)


def add_pair(mine, theirs, out):
    for k in range(CHIPS):
        out[k] = (mine[k] + theirs[k].astype(F32)).astype(BF16)


def finish(received, bo, out):
    odd = lax.axis_index("tp") % 2 == 1
    total = received[0].astype(F32)
    for i in range(1, CHIPS):
        total = total + received[i].astype(F32)
    lane = lanes((ROWS, HD))
    low = jnp.where(
        odd,
        jnp.where(lane < R, total[:, :HD], 0.0),
        jnp.where(lane < R, 0.0, total[:, 2 * HD :]),
    )
    high = low.astype(BF16)
    rest = (low - high.astype(F32)).astype(BF16)
    extra = jnp.dot(high, bo[...], preferred_element_type=F32) + jnp.dot(
        rest, bo[...], preferred_element_type=F32
    )
    moved = pltpu.roll(total, 3 * HD - R, 1)
    result = (jnp.where(odd, moved, total) + 0.5 * extra)[:, :OUT].astype(BF16)
    for s in range(SEQS):
        out[0, s] = result[STEPS * s : STEPS * s + STEPS]


def call(kernel, in_specs, outs, scratch=(), vmem=24):
    single = not isinstance(outs, (list, tuple))
    return pl.pallas_call(
        kernel,
        out_shape=outs,
        in_specs=in_specs,
        out_specs=VMEM if single else [VMEM] * len(outs),
        scratch_shapes=list(scratch),
        cost_estimate=pl.CostEstimate(flops=1_000_000, bytes_accessed=1_000_000, transcendentals=0),
        compiler_params=pltpu.CompilerParams(vmem_limit_bytes=vmem * 1024 * 1024),
    )


def shape(*dims, dtype=BF16):
    return jax.ShapeDtypeStruct(dims, dtype)


def per_device(
    hidden_in,
    q_weight,
    kv_weight,
    o_weight,
    q_gain,
    k_gain,
    cache,
    lengths,
    owner,
    a_q,
    b_q,
    a_o,
    b_o,
):
    tokens = hidden_in.reshape(ROWS, WIDTH)
    other_core = [(i, i ^ 1) for i in range(TP)]
    same_core = [list(range(0, TP, 2)), list(range(1, TP, 2))]
    q_gain, k_gain = q_gain.reshape(1, HD), k_gain.reshape(1, HD)

    message = call(
        pack_factors,
        [HBM] * 4,
        shape(GROUPS, FACTOR_ROWS, HD),
        [
            pltpu.VMEM((R, BLOCK), BF16),
            pltpu.VMEM((4, 2 * HD), BF16),
            pltpu.VMEM((4, 2 * HD), BF16),
            pltpu.VMEM((4, OUT), BF16),
            pltpu.VMEM((BLOCK, HD), F32),
            pltpu.VMEM((FACTOR_ROWS, HD), F32),
            pltpu.SemaphoreType.DMA((4,)),
        ],
        vmem=60,
    )(a_q.T, b_q, a_o.T, b_o)
    factors = lax.all_to_all(message, "group", 0, 0)

    query_part = jnp.dot(tokens, q_weight, preferred_element_type=F32)
    keyval_part = jnp.dot(tokens, kv_weight, preferred_element_type=F32)

    bounds = jnp.broadcast_to(lengths.reshape(SEQS, 1).astype(F32), (SEQS, HD))
    gains = jnp.concatenate([q_gain, k_gain, bounds], axis=0)
    kv_other = lax.ppermute(keyval_part, "tp", other_core)
    low_own = call(
        low_rank,
        [SMEM, VMEM, VMEM, VMEM, VMEM],
        shape(ROWS, HD, dtype=F32),
        [pltpu.VMEM((WIDTH, HD), BF16)],
    )(owner, tokens, factors, kv_other, gains)
    low_other = lax.ppermute(low_own, "tp", other_core)
    bq, ao, bo = call(
        unpack_factors,
        [VMEM],
        [shape(2 * R, 2 * HD), shape(2 * R, 2 * HD), shape(2 * R, 3 * HD)],
        [pltpu.VMEM((R, 3 * HD), F32)],
    )(factors)
    message = call(
        pack_queries,
        [VMEM] * 7,
        shape(CHIPS, QKV_ROWS, HD),
        [pltpu.VMEM((QKV_ROWS, HD), F32)],
    )(query_part, keyval_part, kv_other, low_own, low_other, bq, gains)
    mine = lax.all_to_all(message, "tp", 0, 0, axis_index_groups=same_core)
    cache = call(
        stage_cache,
        [ANY, ANY],
        shape(*cache.shape),
        [pltpu.SemaphoreType.DMA((SEQS,))],
    )(cache, message)
    theirs = lax.ppermute(mine, "tp", other_core)

    own_part, other_part = call(
        cached_attention,
        [VMEM] * 4,
        [shape(CHIPS, PART_ROWS, HD, dtype=F32), shape(CHIPS, PART_ROWS, HD)],
        [
            pltpu.VMEM((TP, 64, HD), F32),
            pltpu.VMEM((TP, PART_ROWS, HD), F32),
            pltpu.VMEM((SEQS, HD, SLOTS), F32),
            pltpu.VMEM((SEQS, HD, SLOTS), BF16),
        ],
    )(gains, mine, theirs, cache)
    other_part = lax.ppermute(other_part, "tp", other_core)
    fresh, fresh_logs = call(
        fresh_attention,
        [VMEM] * 2,
        [shape(64, HD, dtype=F32), shape(PER_SEQ, HD, dtype=F32)],
    )(mine, theirs)

    message = call(merge_parts, [VMEM] * 3, shape(CHIPS, PART_ROWS, HD))(
        own_part, other_part, fresh_logs
    )
    parts = lax.all_to_all(message, "tp", 0, 0, axis_index_groups=same_core)
    theirs, heads, low = call(
        project_theirs,
        [VMEM] * 5,
        [shape(CHIPS, ROWS, 3 * HD), shape(ROWS, 2 * HD), shape(ROWS, HD, dtype=F32)],
        [pltpu.VMEM((ROWS, 2 * HD), F32)],
    )(parts, fresh, fresh_logs, ao, o_weight)
    theirs = lax.ppermute(theirs, "tp", other_core)
    mine = call(
        project_mine,
        [VMEM] * 3,
        shape(CHIPS, ROWS, 3 * HD, dtype=F32),
    )(heads, low, o_weight)
    message = call(add_pair, [VMEM, VMEM], shape(CHIPS, ROWS, 3 * HD))(mine, theirs)
    sums = lax.all_to_all(message, "tp", 0, 0, axis_index_groups=same_core)
    return call(finish, [VMEM, VMEM], shape(1, SEQS, STEPS, OUT))(sums, bo)


def solution(mesh):
    placed = (
        P("group", None, None, None),
        P(None, "tp"),
        P(None, "tp"),
        P("tp", None),
        P(),
        P(),
        P("group", None, None, None, "tp", None),
        P("group", None),
        P(),
        P("group", None),
        P("group", "tp"),
        P("tp", "group"),
        P("group", "tp"),
    )
    return jax.shard_map(
        per_device,
        mesh=mesh,
        in_specs=placed,
        out_specs=P("group", None, None, "tp"),
        check_vma=False,
    )
```

```python
import functools
import math

import jax
import jax.numpy as jnp
from jax import lax
from jax.experimental import pallas as pl
from jax.experimental.pallas import tpu as pltpu
from jax.sharding import PartitionSpec as P

HD = 128
QH = 32
KVH = 4
R = 64
TP = 16
CHIPS = TP // 2
GROUPS = 16
SEQS = 8
STEPS = 4
ROWS = SEQS * STEPS
PER_SEQ = 2 * STEPS
WIDTH = 5120
SLOTS = 256
BLOCK = WIDTH // GROUPS
HALF = BLOCK // 2
OUT = WIDTH // TP
INV_ROOT = 1.0 / math.sqrt(HD)
FAR = -1e30
BF16 = jnp.bfloat16
F32 = jnp.float32

BQ_AT = 80
AO_AT = 88
BO_AT = 96
FACTOR_ROWS = 112
QKV_ROWS = 80
PART_ROWS = 80

VMEM = pl.BlockSpec(memory_space=pltpu.VMEM)
HBM = pl.BlockSpec(memory_space=pltpu.HBM)
ANY = pl.BlockSpec(memory_space=pl.ANY)
SMEM = pl.BlockSpec(memory_space=pltpu.SMEM)
NT = (((1,), (1,)), ((), ()))


def lanes(shape):
    return lax.broadcasted_iota(jnp.int32, shape, len(shape) - 1)


def norm(values, gain):
    mean_square = jnp.mean(values * values, axis=-1, keepdims=True)
    return values * lax.rsqrt(mean_square + 1e-06) * gain


def pack_factors(a_q, b_q, a_o, b_o, out, a_q_in, b_q_in, a_o_in, b_o_in, turned, rows, sems):
    pairs = ((a_q, a_q_in), (b_q, b_q_in), (a_o, a_o_in), (b_o, b_o_in))
    copies = [
        pltpu.make_async_copy(source, place, sems.at[k]) for k, (source, place) in enumerate(pairs)
    ]
    for copy in copies:
        copy.start()
    for copy in copies:
        copy.wait()
    row = lax.broadcasted_iota(jnp.int32, (R, HD), 0)
    unit = jnp.where(lanes((R, HD)) % R == row, 1.0, 0.0).astype(BF16)
    turned[...] = lax.dot_general(
        a_q_in[...], unit, (((0,), (0,)), ((), ())), preferred_element_type=F32
    )
    start = pl.multiple_of((lax.axis_index("tp") % 2) * HALF, HALF)
    first = turned[pl.ds(start, 80), :]
    second = turned[pl.ds(start + 80, 80), :]
    rows[0:80, :] = jnp.where(lanes((80, HD)) < R, first, second)
    bq = b_q_in[...].astype(F32)
    rows[BQ_AT : BQ_AT + 4, :] = bq[:, :HD]
    rows[BQ_AT + 4 : BQ_AT + 8, :] = bq[:, HD:]
    ao = a_o_in[...].astype(F32)
    rows[AO_AT : AO_AT + 4, :] = ao[:, :HD]
    rows[AO_AT + 4 : AO_AT + 8, :] = ao[:, HD:]
    bo = b_o_in[...].astype(F32)
    rows[BO_AT : BO_AT + 4, :] = bo[:, :HD]
    rows[BO_AT + 4 : BO_AT + 8, :] = bo[:, HD : 2 * HD]
    rows[BO_AT + 8 : BO_AT + 16, :] = jnp.zeros((8, HD), F32)
    rows[BO_AT + 8 : BO_AT + 12, 0:64] = bo[:, 2 * HD :]
    message = rows[...].astype(BF16)
    for g in range(GROUPS):
        out[g] = message


def stage_cache(cache, _, out, sems):
    copies = [pltpu.make_async_copy(cache.at[0, s], out.at[0, s], sems.at[s]) for s in range(SEQS)]
    for copy in copies:
        copy.start()
    for copy in copies:
        copy.wait()


def low_rank(owner, tokens, factors, _, __, out, a_true):
    core = lax.axis_index("tp") % 2
    lane = lanes((80, HD))
    left = jnp.where(lane < R, 1.0, 0.0).astype(BF16)
    right = jnp.where(lane < R, 0.0, 1.0).astype(BF16)
    empty = jnp.zeros((HALF, HD), BF16)
    for g in range(GROUPS):
        base = owner[0, g] * BLOCK
        mine = pl.multiple_of(base + core * HALF, 32)
        other = pl.multiple_of(base + (1 - core) * HALF, 32)
        block = factors[g, 0:80, :]
        a_true[pl.ds(mine, 80), :] = block * left
        a_true[pl.ds(pl.multiple_of(mine + 80, 16), 80), :] = block * right
        a_true[pl.ds(other, HALF), :] = empty
    both = jnp.dot(tokens[...], a_true[...], preferred_element_type=F32)
    out[...] = both + pltpu.roll(both, R, 1)


def unpack_factors(factors, bq_out, ao_out, bo_out, rows):
    for at, pieces, out in ((BQ_AT, 2, bq_out), (AO_AT, 2, ao_out), (BO_AT, 3, bo_out)):
        for g in range(GROUPS):
            block = factors[g, BQ_AT:FACTOR_ROWS, :].astype(F32)
            for h in range(pieces):
                piece = block[at - BQ_AT + 4 * h : at - BQ_AT + 4 * h + 4]
                rows[4 * g : 4 * g + 4, HD * h : HD * h + HD] = piece
        whole = rows[:, : HD * pieces].astype(BF16)
        out[0:R, :] = whole
        out[R : 2 * R, :] = whole


def pack_queries(query_part, kv_own, kv_other, low_own, low_other, bq, gains, out, rows):
    chip, core = lax.axis_index("tp") // 2, lax.axis_index("tp") % 2
    low = low_own[...] + low_other[...]
    lane = lanes((ROWS, HD))
    high = low.astype(BF16).astype(F32)
    low_terms = jnp.where(lane < R, high, low - high).astype(BF16)
    query = query_part[...] + 0.5 * jnp.dot(low_terms, bq[...], preferred_element_type=F32)
    for e in range(2):
        normed = norm(query[:, HD * e : HD * e + HD], gains[0:1, :])
        for s in range(SEQS):
            at = PER_SEQ * s + STEPS * e
            rows[at : at + STEPS, :] = normed[STEPS * s : STEPS * s + STEPS]
    own, other = kv_own[...], kv_other[...]
    left, right = jnp.where(core == 0, own, other), jnp.where(core == 0, other, own)
    head = jnp.concatenate([left, right], axis=1)
    head = jnp.where(chip < KVH, norm(head, gains[1:2, :]), head)
    rows[64:80, :] = jnp.where(core == 0, head[0:16], head[16:32])
    message = rows[...].astype(BF16)
    for i in range(CHIPS):
        out[i] = message


def cached_attention(
    gains, mine, theirs, cache, own_part, other_part, queries, weighted, scores, weights
):
    first = lax.axis_index("tp") * SLOTS
    core = lax.axis_index("tp") % 2
    for i in range(CHIPS):
        queries[2 * i + core] = mine[i, 0:64, :].astype(F32)
        queries[2 * i + 1 - core] = theirs[i, 0:64, :].astype(F32)
    position = (lanes((HD, SLOTS)) + first).astype(F32)
    lane = lanes((HD, HD))
    for s in range(SEQS):
        query = queries[:, PER_SEQ * s : PER_SEQ * s + PER_SEQ, :].reshape(HD, HD).astype(BF16)
        for c in range(KVH):
            scores[s, ROWS * c : ROWS * c + ROWS, :] = lax.dot_general(
                query[ROWS * c : ROWS * c + ROWS],
                cache[0, s, 0, c],
                NT,
                preferred_element_type=F32,
            )
    logs = jnp.zeros((HD, HD), F32)
    inverse = []
    for s in range(SEQS):
        bound = jnp.concatenate([gains[2 + s : 3 + s, :]] * 2, axis=1)
        score = jnp.where(position < bound, scores[s] * INV_ROOT, FAR)
        largest = score.max(axis=-1, keepdims=True)
        weight = jnp.exp(score - largest)
        total = weight.sum(axis=-1, keepdims=True)
        weights[s] = weight.astype(BF16)
        log = jnp.where(largest > 0.5 * FAR, largest + jnp.log(total), FAR)
        logs = jnp.where(lane % SEQS == s, log, logs)
        inverse.append(1.0 / total)
    for s in range(SEQS):
        value = [
            jnp.dot(
                weights[s, ROWS * c : ROWS * c + ROWS, :],
                cache[0, s, 1, c],
                preferred_element_type=F32,
            )
            for c in range(KVH)
        ]
        value = jnp.concatenate(value, axis=0) * inverse[s]
        weighted[:, PER_SEQ * s : PER_SEQ * s + PER_SEQ, :] = value.reshape(TP, PER_SEQ, HD)
    high = logs.astype(BF16).astype(F32)
    middle = (logs - high).astype(BF16).astype(F32)
    terms = jnp.where(lane < 8, high, jnp.where(lane < 16, middle, logs - high - middle))
    weighted[:, 64:72, :] = terms.reshape(TP, PER_SEQ, HD)
    weighted[:, 72:80, :] = jnp.zeros((TP, 8, HD), F32)
    for i in range(CHIPS):
        own_part[i] = weighted[2 * i + core]
        other_part[i] = weighted[2 * i + 1 - core].astype(BF16)


def log_sum(terms):
    return terms + pltpu.roll(terms, HD - 8, 1) + pltpu.roll(terms, HD - 16, 1)


def spread(shares):
    rows = shares.shape[0]
    high = shares.astype(BF16).astype(F32)
    low = pltpu.roll(shares - high, SEQS, 1)
    terms = jnp.where(lanes((rows, HD)) < SEQS, high, low).astype(BF16)[:, : 2 * SEQS]
    row = lax.broadcasted_iota(jnp.int32, (2 * SEQS, SEQS * HD), 0)
    unit = jnp.where(row % SEQS == lanes((2 * SEQS, SEQS * HD)) // HD, 1.0, 0.0).astype(BF16)
    return jnp.dot(terms, unit, preferred_element_type=F32)


def merge_parts(own, other, _, out):
    lane = lanes((64, HD))
    theirs = [other[i].astype(F32) for i in range(CHIPS)]
    logs = [
        log_sum(jnp.concatenate([own[i, 64:72, :] for i in range(CHIPS)], axis=0)),
        log_sum(jnp.concatenate([part[64:72] for part in theirs], axis=0)),
    ]
    largest = jnp.maximum(logs[0], logs[1])
    shares = [jnp.exp(log - largest) for log in logs]
    total = shares[0] + shares[1]
    inverse = 1.0 / total
    wide = spread(jnp.concatenate([shares[0] * inverse, shares[1] * inverse], axis=0))
    log = largest + jnp.log(total)
    high = log.astype(BF16).astype(F32)
    middle = (log - high).astype(BF16).astype(F32)
    low = log - high - middle
    terms = jnp.where(lane < 16, pltpu.roll(middle, 8, 1), pltpu.roll(low, 16, 1))
    terms = jnp.where(lane < 8, high, terms)
    for i in range(CHIPS):
        at = PER_SEQ * i
        rows = []
        for s in range(SEQS):
            block = slice(HD * s, HD * s + HD)
            rows.append(
                own[i, PER_SEQ * s : PER_SEQ * s + PER_SEQ, :] * wide[at : at + PER_SEQ, block]
                + theirs[i][PER_SEQ * s : PER_SEQ * s + PER_SEQ]
                * wide[64 + at : 64 + at + PER_SEQ, block]
            )
        rows.append(terms[at : at + PER_SEQ])
        rows.append(jnp.zeros((PER_SEQ, HD), F32))
        out[i] = jnp.concatenate(rows, axis=0).astype(BF16)


def fresh_attention(mine, theirs, out, logs):
    chip, core = lax.axis_index("tp") // 2, lax.axis_index("tp") % 2
    head = chip // (CHIPS // KVH)

    def whole(at):
        own, other = mine[at, 64:80, :].astype(F32), theirs[at, 64:80, :].astype(F32)
        low, high = jnp.where(core == 0, own, other), jnp.where(core == 0, other, own)
        return jnp.concatenate([low, high], axis=0).astype(BF16)

    keys, values = whole(head), whole(KVH + head)
    scores = (
        lax.dot_general(mine[chip, 0:64, :], keys, NT, preferred_element_type=F32) * INV_ROOT
    )
    row = lax.broadcasted_iota(jnp.int32, (64, ROWS), 0)
    column = lanes((64, ROWS))
    seen = (row // PER_SEQ == column // STEPS) & (row % STEPS >= column % STEPS)
    scores = jnp.where(seen, scores, FAR)
    largest = scores.max(axis=-1, keepdims=True)
    weights = jnp.where(seen, jnp.exp(scores - largest), 0.0)
    total = weights.sum(axis=-1, keepdims=True)
    value = jnp.dot(weights.astype(BF16), values, preferred_element_type=F32)
    out[...] = value / total
    log = largest + jnp.log(total)
    lane = lanes((PER_SEQ, HD))
    compact = jnp.zeros((PER_SEQ, HD), F32)
    for s in range(SEQS):
        compact = jnp.where(lane == s, log[PER_SEQ * s : PER_SEQ * s + PER_SEQ], compact)
    logs[...] = compact


def place_columns(heads, low, o_in, core, out):
    lane = lanes((ROWS, HD))
    for k in range(CHIPS):
        start = pl.multiple_of(2 * OUT * k + 2 * HD * core, HD)
        value = jnp.dot(heads, o_in[:, pl.ds(start, 3 * HD)], preferred_element_type=F32)
        first, last = value[:, :HD], value[:, 2 * HD :]
        first = jnp.where((lane < R) & (core == 1), low, first)
        last = jnp.where((lane >= R) & (core == 0), low, last)
        out[k, :, 0:HD] = first.astype(out.dtype)
        out[k, :, HD : 2 * HD] = value[:, HD : 2 * HD].astype(out.dtype)
        out[k, :, 2 * HD :] = last.astype(out.dtype)


def project_theirs(
    received, fresh, fresh_logs, ao, o_in, theirs, heads, low, attended
):
    logs = []
    for i in range(CHIPS):
        logs.append(log_sum(received[i, 64:80, :].astype(F32)[0:8]))
    logs.append(fresh_logs[...])
    largest = functools.reduce(jnp.maximum, logs)
    shares = [jnp.exp(log - largest) for log in logs]
    inverse = 1.0 / functools.reduce(jnp.add, shares)
    wide = spread(jnp.concatenate([share * inverse for share in shares], axis=0))
    for pair in range(SEQS // 2):
        blocks = [received[i, 16 * pair : 16 * pair + 16, :].astype(F32) for i in range(CHIPS)]
        for s in (2 * pair, 2 * pair + 1):
            at, block = PER_SEQ * s, slice(HD * s, HD * s + HD)
            total = fresh[at : at + PER_SEQ, :] * wide[64:72, block]
            for i in range(CHIPS):
                part = blocks[i][at - 16 * pair : at - 16 * pair + PER_SEQ]
                total = total + part * wide[PER_SEQ * i : PER_SEQ * i + PER_SEQ, block]
            for e in range(2):
                attended[STEPS * s : STEPS * s + STEPS, HD * e : HD * e + HD] = total[
                    STEPS * e : STEPS * e + STEPS
                ]
    heads[...] = attended[...].astype(BF16)
    low[...] = lax.dot_general(heads[...], ao[...], NT, preferred_element_type=F32)
    place_columns(heads[...], low[...], o_in, 1 - lax.axis_index("tp") % 2, theirs)


def project_mine(heads, low, o_in, mine):
    place_columns(heads[...], low[...], o_in, lax.axis_index("tp") % 2, mine)


def add_pair(mine, theirs, out):
    for k in range(CHIPS):
        out[k] = (mine[k] + theirs[k].astype(F32)).astype(BF16)


def finish(received, bo, out):
    odd = lax.axis_index("tp") % 2 == 1
    total = received[0].astype(F32)
    for i in range(1, CHIPS):
        total = total + received[i].astype(F32)
    lane = lanes((ROWS, HD))
    low = jnp.where(
        odd,
        jnp.where(lane < R, total[:, :HD], 0.0),
        jnp.where(lane < R, 0.0, total[:, 2 * HD :]),
    )
    high = low.astype(BF16)
    rest = (low - high.astype(F32)).astype(BF16)
    extra = jnp.dot(high, bo[...], preferred_element_type=F32) + jnp.dot(
        rest, bo[...], preferred_element_type=F32
    )
    moved = pltpu.roll(total, 3 * HD - R, 1)
    result = (jnp.where(odd, moved, total) + 0.5 * extra)[:, :OUT].astype(BF16)
    for s in range(SEQS):
        out[0, s] = result[STEPS * s : STEPS * s + STEPS]


def call(kernel, in_specs, outs, scratch=(), vmem=24):
    single = not isinstance(outs, (list, tuple))
    return pl.pallas_call(
        kernel,
        out_shape=outs,
        in_specs=in_specs,
        out_specs=VMEM if single else [VMEM] * len(outs),
        scratch_shapes=list(scratch),
        cost_estimate=pl.CostEstimate(flops=1_000_000, bytes_accessed=1_000_000, transcendentals=0),
        compiler_params=pltpu.CompilerParams(vmem_limit_bytes=vmem * 1024 * 1024),
    )


def shape(*dims, dtype=BF16):
    return jax.ShapeDtypeStruct(dims, dtype)


def per_device(
    hidden_in,
    q_weight,
    kv_weight,
    o_weight,
    q_gain,
    k_gain,
    cache,
    lengths,
    owner,
    a_q,
    b_q,
    a_o,
    b_o,
):
    tokens = hidden_in.reshape(ROWS, WIDTH)
    other_core = [(i, i ^ 1) for i in range(TP)]
    same_core = [list(range(0, TP, 2)), list(range(1, TP, 2))]
    q_gain, k_gain = q_gain.reshape(1, HD), k_gain.reshape(1, HD)

    message = call(
        pack_factors,
        [HBM] * 4,
        shape(GROUPS, FACTOR_ROWS, HD),
        [
            pltpu.VMEM((R, BLOCK), BF16),
            pltpu.VMEM((4, 2 * HD), BF16),
            pltpu.VMEM((4, 2 * HD), BF16),
            pltpu.VMEM((4, OUT), BF16),
            pltpu.VMEM((BLOCK, HD), F32),
            pltpu.VMEM((FACTOR_ROWS, HD), F32),
            pltpu.SemaphoreType.DMA((4,)),
        ],
        vmem=60,
    )(a_q.T, b_q, a_o.T, b_o)
    factors = lax.all_to_all(message, "group", 0, 0)

    query_part = jnp.dot(tokens, q_weight, preferred_element_type=F32)
    keyval_part = jnp.dot(tokens, kv_weight, preferred_element_type=F32)

    bounds = jnp.broadcast_to(lengths.reshape(SEQS, 1).astype(F32), (SEQS, HD))
    gains = jnp.concatenate([q_gain, k_gain, bounds], axis=0)
    kv_other = lax.ppermute(keyval_part, "tp", other_core)
    low_own = call(
        low_rank,
        [VMEM] * 5,
        shape(ROWS, HD, dtype=F32),
        [pltpu.VMEM((WIDTH, HD), BF16)],
    )(owner.reshape(1, GROUPS), tokens, factors, kv_other, gains)
    low_other = lax.ppermute(low_own, "tp", other_core)
    bq, ao, bo = call(
        unpack_factors,
        [VMEM],
        [shape(2 * R, 2 * HD), shape(2 * R, 2 * HD), shape(2 * R, 3 * HD)],
        [pltpu.VMEM((R, 3 * HD), F32)],
    )(factors)
    message = call(
        pack_queries,
        [VMEM] * 7,
        shape(CHIPS, QKV_ROWS, HD),
        [pltpu.VMEM((QKV_ROWS, HD), F32)],
    )(query_part, keyval_part, kv_other, low_own, low_other, bq, gains)
    mine = lax.all_to_all(message, "tp", 0, 0, axis_index_groups=same_core)
    cache = call(
        stage_cache,
        [ANY, ANY],
        shape(*cache.shape),
        [pltpu.SemaphoreType.DMA((SEQS,))],
    )(cache, message)
    theirs = lax.ppermute(mine, "tp", other_core)

    own_part, other_part = call(
        cached_attention,
        [VMEM] * 4,
        [shape(CHIPS, PART_ROWS, HD, dtype=F32), shape(CHIPS, PART_ROWS, HD)],
        [
            pltpu.VMEM((TP, 64, HD), F32),
            pltpu.VMEM((TP, PART_ROWS, HD), F32),
            pltpu.VMEM((SEQS, HD, SLOTS), F32),
            pltpu.VMEM((SEQS, HD, SLOTS), BF16),
        ],
    )(gains, mine, theirs, cache)
    other_part = lax.ppermute(other_part, "tp", other_core)
    fresh, fresh_logs = call(
        fresh_attention,
        [VMEM] * 2,
        [shape(64, HD, dtype=F32), shape(PER_SEQ, HD, dtype=F32)],
    )(mine, theirs)

    message = call(merge_parts, [VMEM] * 3, shape(CHIPS, PART_ROWS, HD))(
        own_part, other_part, fresh_logs
    )
    parts = lax.all_to_all(message, "tp", 0, 0, axis_index_groups=same_core)
    theirs, heads, low = call(
        project_theirs,
        [VMEM] * 5,
        [shape(CHIPS, ROWS, 3 * HD), shape(ROWS, 2 * HD), shape(ROWS, HD, dtype=F32)],
        [pltpu.VMEM((ROWS, 2 * HD), F32)],
    )(parts, fresh, fresh_logs, ao, o_weight)
    theirs = lax.ppermute(theirs, "tp", other_core)
    mine = call(
        project_mine,
        [VMEM] * 3,
        shape(CHIPS, ROWS, 3 * HD, dtype=F32),
    )(heads, low, o_weight)
    message = call(add_pair, [VMEM, VMEM], shape(CHIPS, ROWS, 3 * HD))(mine, theirs)
    sums = lax.all_to_all(message, "tp", 0, 0, axis_index_groups=same_core)
    return call(finish, [VMEM, VMEM], shape(1, SEQS, STEPS, OUT))(sums, bo)


def solution(mesh):
    placed = (
        P("group", None, None, None),
        P(None, "tp"),
        P(None, "tp"),
        P("tp", None),
        P(),
        P(),
        P("group", None, None, None, "tp", None),
        P("group", None),
        P(),
        P("group", None),
        P("group", "tp"),
        P("tp", "group"),
        P("group", "tp"),
    )
    return jax.shard_map(
        per_device,
        mesh=mesh,
        in_specs=placed,
        out_specs=P("group", None, None, "tp"),
        check_vma=False,
    )
```
